128 devices in a mesh: expert: 8 (over x_lo, y), fsdp: 16 (over z, x_hi, core).
Axes of the slice: x: 4 (x_hi: 2, x_lo: 2; x = x_hi * 2 + x_lo), y: 4, z: 4, core: 2. Of those that a mesh axis runs over, the one named last changes fastest.
Arguments:
- tokens: bfloat16 [8192, 3072], P(('expert', 'fsdp')), may hold values from -6 to 6
- expert_ids: int32 [8192, 2], P(('expert', 'fsdp')), may hold values from 0 to 7, all different within a row; in each aligned block of 64 rows (0 to 63, 64 to 127, ...) at most 18 rows name the same one
- route_weights: float32 [8192, 2], P(('expert', 'fsdp')), may hold values from 0.2 to 1
- up_weight: bfloat16 [8, 16384, 3072], P('expert', 'fsdp'), may hold values from -0.109375 to 0.109375
- down_weight: bfloat16 [8, 16384, 3072], P('expert', 'fsdp'), may hold values from -0.046875 to 0.046875
Outputs:
- mixed: bfloat16 [8192, 3072], P(('expert', 'fsdp'))
The draws below stay inside these ranges and needn't reach their ends.
Inputs may be any that keep to these rules, and one draw needn't show every extreme that they name: `expert_ids`: each row names 2 different experts. Within the rows of one device (aligned blocks of 64 rows) no expert is named by more than 18 rows, and in every block some expert is named by exactly 18 rows.
All inputs are finite; a program needn't handle non-finite values.
Results may differ from the reference program's by a relative error of at most 0.019.
Values may be sent and summed in bfloat16 or wider, within the bound.
A program may use at most 128 MiB of HBM per device.

```python
import math
import jax
import jax.numpy as jnp
import numpy as np
from jax import lax

D = 3072
FF = 16384
TOPK = 2
TOK_DEV = 64
EXPERTS = 8
CAP = 18
TOKENS = 8192
N_FSDP = 16


def block_levels(stream_key, shape, pieces, least, largest):
    loudness, own = 1.0, jax.random.fold_in(stream_key, 6)
    for position, shards_of in pieces:
        steps = jnp.exp(jax.random.uniform(jax.random.fold_in(own, position), (shards_of,), jnp.float32, least / len(pieces), largest / len(pieces)))
        loudness = loudness * jnp.repeat(steps, shape[position] // shards_of).reshape([-1 if axis == position else 1 for axis in range(len(shape))])
    return loudness


def deal_out(own_key, own, number, rows, amount, top, bound, slope):
    ranking = jax.random.permutation(own_key, amount)
    crowded, usual = shares(amount, rows * top, bound, slope, True), shares(amount, rows * top, bound, slope, False)
    places = jnp.arange(amount)

    def named(sizes, turn):
        used = int((sizes > 0).sum())
        fixed = max(1, used // 4)
        passed = fixed + (places - fixed + turn * (used - fixed)) % max(1, amount - fixed)
        return jnp.zeros((amount,), jnp.int32).at[ranking[jnp.where(places < fixed, places, passed)]].set(jnp.asarray(sizes, jnp.int32))

    sizes = jnp.where(number % 4 == 0, named(crowded, number // 4), named(usual, number - number // 4 - 1))
    mixed = jax.random.permutation(jax.random.fold_in(own, 3), amount)
    donor, receiver = mixed[0:amount // 2 * 2:2], mixed[1:amount // 2 * 2:2]
    margin = jnp.minimum(sizes[donor] - 1, bound - sizes[receiver]) // 2
    margin = jnp.where((donor == ranking[0]) | (receiver == ranking[0]) | (sizes[receiver] == 0), 0, jnp.maximum(margin, 0))
    passed = jax.random.randint(jax.random.fold_in(own, 4), (amount // 2,), 0, 1 << 20) % (margin + 1)
    sizes = sizes.at[donor].add(-passed).at[receiver].add(passed)
    members = jnp.searchsorted(jnp.cumsum(sizes), jnp.arange(rows * top), side="right").astype(jnp.int32)
    grid = members.reshape(top, rows).T
    grid = grid[jax.random.permutation(jax.random.fold_in(own, 1), rows)]
    turn = jax.random.randint(jax.random.fold_in(own, 2), (rows, 1), 0, top)
    return jnp.take_along_axis(grid, (jnp.arange(top)[None, :] + turn) % top, axis=1)


def shares(count, total, reach, lean, full):
    weights = [(1 << 20) // math.isqrt(rank ** lean) + 1 for rank in range(1, count + 1)]
    largest = reach if full else min(reach, max(-(-total // count), total * weights[0] // sum(weights)))
    least = 1 if total - largest >= count - 1 else 0
    given, surplus = [largest] + [least] * (count - 1), total - largest - least * (count - 1)
    while surplus > 0:
        free = [i for i in range(1, count) if given[i] < largest] or [i for i in range(1, count) if given[i] < reach]
        mass, budget = sum([weights[i] for i in free]), surplus
        for i in free:
            extra = min(reach - given[i], max(1, budget * weights[i] // mass), surplus)
            given[i] = given[i] + extra
            surplus = surplus - extra
    return np.array(given)


def noise(own_key, extent, scale, most, split=(), kind=jnp.bfloat16):
    gain = block_levels(own_key, extent, split, -0.22, 0.18) if split else 1.0
    values = jax.random.normal(own_key, extent, jnp.float32) * scale * gain
    return jnp.minimum(jnp.maximum(values, -most), most).astype(kind)


def setup_inputs(seed: int = 0) -> dict:
    streams_of = jax.random.split(jax.random.key(seed), 6)
    tokens = noise(streams_of[0], (TOKENS, D), 1.0, 6.0, ((0, 128),))
    expert_ids_keys = jax.random.split(jax.random.fold_in(streams_of[1], 1), TOKENS // TOK_DEV)
    expert_ids_turns = jax.random.permutation(jax.random.fold_in(streams_of[1], 3), TOKENS // TOK_DEV)
    expert_ids = jax.vmap(lambda own, number: deal_out(jax.random.fold_in(streams_of[1], 2), own, number, TOK_DEV, EXPERTS, TOPK, CAP, 1))(expert_ids_keys, expert_ids_turns).reshape((TOKENS, TOPK))
    route_weights = jnp.clip(0.2 + 0.8 * jax.random.uniform(streams_of[2], (TOKENS, TOPK), jnp.float32) ** block_levels(streams_of[2], (TOKENS, TOPK), ((0, 128),), -0.2, 0.2), 0.2, 1.0)
    up_weight = noise(streams_of[3], (EXPERTS, FF, D), D ** -0.5, 0.109375, ((0, 8), (1, 16)))
    down_weight = noise(streams_of[4], (EXPERTS, FF, D), FF ** -0.5, 0.046875, ((0, 8), (1, 16)))
    return dict(tokens=tokens, expert_ids=expert_ids, route_weights=route_weights, up_weight=up_weight, down_weight=down_weight)


def reference(tokens, expert_ids, route_weights, up_weight, down_weight):
    blocks = TOKENS // TOK_DEV
    id_grid = expert_ids.reshape(blocks, TOK_DEV, TOPK)
    numbers = jnp.arange(EXPERTS, dtype=jnp.int32)
    chosen = (id_grid[..., None] == numbers).astype(jnp.int32)
    counts = chosen.sum(2)
    before = jnp.cumsum(counts, axis=1) - counts
    slot_index = jnp.sum(chosen * before[:, :, None, :], axis=3)
    block_start = jnp.arange(blocks, dtype=jnp.int32)[:, None, None] * CAP
    target = (block_start + slot_index).reshape(TOKENS, TOPK).astype(jnp.int32)
    slot_rows = blocks * CAP
    shard_width = FF // N_FSDP

    def one_expert(expert):
        placed = jnp.where(expert_ids == expert, target, slot_rows).astype(jnp.int32)
        expert_rows = jnp.zeros((slot_rows, D), jnp.bfloat16)
        expert_rows = expert_rows.at[placed[:, 0]].set(tokens, mode="drop")
        expert_rows = expert_rows.at[placed[:, 1]].set(tokens, mode="drop")
        up_rows = lax.dynamic_index_in_dim(up_weight, expert, 0, keepdims=False)
        down_rows = lax.dynamic_index_in_dim(down_weight, expert, 0, keepdims=False)
        up_blocks = up_rows.reshape(N_FSDP, shard_width, D)
        down_blocks = down_rows.reshape(N_FSDP, shard_width, D)

        def add_block(total, panels):
            up_block, down_block = panels
            activated = jax.nn.silu(lax.dot_general(expert_rows, up_block, (((1,), (1,)), ((), ())), preferred_element_type=jnp.float32)).astype(jnp.bfloat16)
            portion = jnp.dot(activated, down_block, preferred_element_type=jnp.float32).astype(jnp.bfloat16)
            return total + lax.optimization_barrier(portion).astype(jnp.float32), None

        total, _ = lax.scan(add_block, jnp.zeros((slot_rows, D), jnp.float32), (up_blocks, down_blocks))
        return total.astype(jnp.bfloat16)

    outputs = lax.map(one_expert, numbers)
    picked = outputs[expert_ids, target]
    combined = jnp.sum(route_weights[:, :, None] * picked.astype(jnp.float32), axis=1)
    return combined.astype(jnp.bfloat16)
```

```python
import functools

import jax
import jax.numpy as jnp
from jax import lax
from jax.experimental import pallas as pl
from jax.experimental.pallas import tpu as pltpu
from jax.sharding import PartitionSpec as P

MESH = pl.DeviceIdType.MESH
BF16, F32 = jnp.bfloat16, jnp.float32

OFFSETS = (
    (0, 0), (1, 0), (3, 0), (0, 1),
    (0, 3), (2, 0), (0, 2), (1, 1),
    (3, 3), (1, 3), (3, 1), (2, 1),
    (1, 2), (2, 3), (3, 2), (2, 2),
)
PEERS = len(OFFSETS)
TILE = 16
EXTRA = 2
GROUPS = TILE // EXTRA
PIECES = 4
PIECE = PEERS // PIECES * TILE
PLANE = PEERS * TILE
REST = PEERS * EXTRA
ROWS = PLANE + REST
TILE_N = 256
WAY_A, WAY_B = (0, 1), (2, 3)


def iota(shape, dim):
    return lax.broadcasted_iota(jnp.int32, shape, dim)


def onehot(mask):
    return jnp.where(mask, 1.0, 0.0).astype(BF16)


def kernel(
    tok_ref, ids_ref, rw_ref, up_ref, down_ref, out_ref,
    up_v, down_v, x_v, y_v, from_up, from_down, far_v, back_v, send_v, hid_v, perm_v, permt_v,
    sem_w, sem_ws, sem_wr, sem_self, sem_ps, sem_pr, sem_as, sem_ar, sem_fs, sem_fr,
    sem_2s, sem_2r, sem_1s, sem_1r, sem_bs, sem_br,
):
    tok_rows, features = tok_ref.shape
    units = up_ref.shape[0]
    fold = features // GROUPS
    e, f = lax.axis_index("expert"), lax.axis_index("fsdp")
    x_lo, y = e // 4, e % 4
    z, x_hi, core = f // 4, (f // 2) % 2, f % 2
    x = x_hi * 2 + x_lo

    def device(dx, dy, dz=0, dc=0):
        px, py, pz, pc = (x + dx) % 4, (y + dy) % 4, (z + dz) % 4, (core + dc) % 2
        return {"expert": (px % 2) * 4 + py, "fsdp": (pz * 2 + px // 2) * 2 + pc}

    peers = [device(dx, dy) for dx, dy in OFFSETS]
    backs = [device(-dx, -dy) for dx, dy in OFFSETS]
    above, below, twin = device(0, 0, 1), device(0, 0, -1), device(0, 0, 0, 1)

    barrier = pltpu.get_barrier_semaphore()
    greeted = peers[1:] + [above, below, twin]
    for other in greeted:
        pl.semaphore_signal(barrier, inc=1, device_id=other, device_id_type=MESH)

    own_up = pltpu.make_async_copy(up_ref, up_v.at[pl.ds(0, units)], sem_w.at[0])
    own_down = pltpu.make_async_copy(down_ref, down_v.at[pl.ds(0, units)], sem_w.at[1])
    own_up.start()
    own_down.start()

    ids = ids_ref[...]
    id0, id1 = ids[:, 0:1], ids[:, 1:2]
    lanes = iota((tok_rows, 128), 1)
    chosen = onehot((id0 == lanes) | (id1 == lanes))
    earlier = onehot(iota((tok_rows, tok_rows), 1) < iota((tok_rows, tok_rows), 0))
    before = jnp.dot(earlier, chosen, preferred_element_type=F32)
    slot0 = jnp.sum(jnp.where(id0 == lanes, before, 0.0), axis=1, keepdims=True).astype(jnp.int32)
    slot1 = jnp.sum(jnp.where(id1 == lanes, before, 0.0), axis=1, keepdims=True).astype(jnp.int32)

    blocks = 8
    wide = blocks * TILE
    place = iota((tok_rows, wide), 1)
    block, within = place // TILE, place % TILE
    expert_of = ((x + block // 4) % 2) * 4 + (y + block % 4) % 4
    in0, in1 = id0 == expert_of, id1 == expert_of
    pick_main = onehot((in0 & (slot0 == within)) | (in1 & (slot1 == within)))
    last = TILE + within % EXTRA
    pick_extra = (in0 & (slot0 == last)) | (in1 & (slot1 == last))
    tokens = tok_ref[...]
    rows_first = (((0,), (0,)), ((), ()))
    send_v[:, :features] = lax.dot_general(pick_main, tokens, rows_first, preferred_element_type=F32).astype(BF16)
    extra = jnp.zeros((wide, fold), F32)
    for g in range(GROUPS):
        extra += lax.dot_general(
            onehot(pick_extra & (within // EXTRA == g)), tok_ref[:, g * fold:(g + 1) * fold],
            rows_first, preferred_element_type=F32)
    send_v[:, features:] = extra.astype(BF16)

    pl.semaphore_wait(barrier, len(greeted))

    def block_of(r):
        dx, dy = OFFSETS[r]
        return (dx % 2) * 4 + dy

    keep = pltpu.make_async_copy(send_v.at[pl.ds(0, TILE)], x_v.at[0, pl.ds(0, TILE)], sem_self.at[0])
    keep.start()
    out_copies = [
        pltpu.make_async_remote_copy(
            src_ref=send_v.at[pl.ds(block_of(r) * TILE, TILE)], dst_ref=x_v.at[0, pl.ds(r * TILE, TILE)],
            send_sem=sem_ps.at[r], recv_sem=sem_pr.at[r], device_id=peers[r], device_id_type=MESH)
        for r in range(1, PEERS)
    ]
    for copy in out_copies:
        copy.start()

    twin_copies = [
        pltpu.make_async_remote_copy(
            src_ref=src, dst_ref=dst.at[pl.ds(units, units)], send_sem=sem_ws.at[i], recv_sem=sem_wr.at[i],
            device_id=twin, device_id_type=MESH)
        for i, (src, dst) in enumerate(((up_ref, up_v), (down_ref, down_v)))
    ]
    for copy in twin_copies:
        copy.start()

    out_row, in_row = iota((PLANE, PLANE), 0), iota((PLANE, PLANE), 1)
    perm_v[...] = onehot(in_row == (out_row % REST) // EXTRA * TILE + out_row // REST * EXTRA + out_row % EXTRA)
    permt_v[...] = onehot(out_row == (in_row % REST) // EXTRA * TILE + in_row // REST * EXTRA + in_row % EXTRA)

    def piece(k):
        return pl.ds(k * PIECE, PIECE)

    def link(src, dst, send, recv, to):
        return pltpu.make_async_remote_copy(
            src_ref=src, dst_ref=dst, send_sem=send, recv_sem=recv, device_id=to, device_id_type=MESH)

    up_copies = [link(x_v.at[0, piece(k)], x_v.at[3, piece(k)], sem_as.at[0, k], sem_ar.at[0, k], above) for k in range(PIECES)]
    down_copies = [link(x_v.at[0, piece(k)], x_v.at[1, piece(k)], sem_as.at[1, k], sem_ar.at[1, k], below) for k in range(PIECES)]
    on_up = [link(x_v.at[3, piece(k)], x_v.at[2, piece(k)], sem_fs.at[k], sem_fr.at[k], above) for k in WAY_A]
    on_down = [link(x_v.at[1, piece(k)], x_v.at[2, piece(k)], sem_fs.at[k], sem_fr.at[k], below) for k in WAY_B]

    for k in range(PIECES):
        for r in range(k * PEERS // PIECES, (k + 1) * PEERS // PIECES):
            if r == 0:
                keep.wait()
            else:
                out_copies[r - 1].wait_recv()
        up_copies[k].start()
        down_copies[k].start()

    def unfold(j):
        moved = jnp.dot(perm_v[...], x_v[j, 0:PLANE, features:], preferred_element_type=F32).astype(BF16)
        for g in range(GROUPS):
            x_v[j, PLANE:ROWS, g * fold:(g + 1) * fold] = moved[g * REST:(g + 1) * REST]

    def refold(j):
        total = jnp.zeros((PLANE, fold), F32)
        for g in range(GROUPS):
            total += jnp.dot(permt_v[:, g * REST:(g + 1) * REST], y_v[j, PLANE:ROWS, g * fold:(g + 1) * fold],
                             preferred_element_type=F32)
        y_v[j, 0:PLANE, features:] = total.astype(BF16)

    def into_hidden(j, first, count):
        def body(n, carry):
            at = pl.ds(pl.multiple_of(n * TILE_N, TILE_N), TILE_N)
            v = lax.dot_general(x_v[j, :, :features], up_v[at, :], (((1,), (1,)), ((), ())), preferred_element_type=F32)
            hid_v[:, at] = (v / (1.0 + jnp.exp(-v))).astype(BF16)
            return carry

        lax.fori_loop(first // TILE_N, (first + count) // TILE_N, body, 0)

    def out_of_hidden(j):
        def body(n, carry):
            at = pl.ds(pl.multiple_of(n * TILE_N, TILE_N), TILE_N)
            y_v[j, :, at] = jnp.dot(hid_v[...], down_v[:, at], preferred_element_type=F32).astype(BF16)
            return carry

        lax.fori_loop(0, features // TILE_N, body, 0)

    unfold(0)
    own_up.wait()
    into_hidden(0, 0, units)
    twin_copies[0].wait_recv()
    into_hidden(0, units, units)
    own_down.wait()
    twin_copies[1].wait_recv()
    out_of_hidden(0)
    refold(0)

    for i in range(len(WAY_A)):
        up_copies[WAY_A[i]].wait_recv()
        on_up[i].start()
    for k in range(PIECES):
        down_copies[k].wait_recv()
        if k in WAY_B:
            on_down[WAY_B.index(k)].start()
    for k in WAY_B:
        up_copies[k].wait_recv()

    to_above = [link(y_v.at[1, piece(k)], from_down.at[piece(k)], sem_1s.at[0, k], sem_1r.at[0, k], above) for k in range(PIECES)]
    to_below = [link(y_v.at[3, piece(k)], from_up.at[piece(k)], sem_1s.at[1, k], sem_1r.at[1, k], below) for k in range(PIECES)]
    far_below = [link(y_v.at[2, piece(k)], far_v.at[piece(k)], sem_2s.at[k], sem_2r.at[k], below) for k in WAY_A]
    far_above = [link(y_v.at[2, piece(k)], far_v.at[piece(k)], sem_2s.at[k], sem_2r.at[k], above) for k in WAY_B]

    def whole(j):
        unfold(j)
        into_hidden(j, 0, 2 * units)
        out_of_hidden(j)
        refold(j)

    whole(1)
    for k in WAY_A:
        to_above[k].start()
    whole(3)
    for k in WAY_B:
        to_below[k].start()
    for copy in on_up + on_down:
        copy.wait_recv()
    whole(2)
    for copy in far_below + far_above:
        copy.start()

    def add_into(target, j, k, others):
        total = target[j, piece(k), :].astype(F32)
        for other in others:
            total += other[piece(k), :].astype(F32)
        target[j, piece(k), :] = total.astype(BF16)

    for i in range(len(WAY_A)):
        far_below[i].wait_recv()
        add_into(y_v, 3, WAY_A[i], (far_v,))
        to_below[WAY_A[i]].start()
        far_above[i].wait_recv()
        add_into(y_v, 1, WAY_B[i], (far_v,))
        to_above[WAY_B[i]].start()

    back_keep = pltpu.make_async_copy(y_v.at[0, pl.ds(0, TILE)], back_v.at[pl.ds(0, TILE)], sem_self.at[1])
    back_copies = [
        link(y_v.at[0, pl.ds(r * TILE, TILE)], back_v.at[pl.ds(r * TILE, TILE)], sem_bs.at[r], sem_br.at[r], backs[r])
        for r in range(1, PEERS)
    ]
    for k in (0, 2, 1, 3):
        to_above[k].wait_recv()
        to_below[k].wait_recv()
        add_into(y_v, 0, k, (from_up, from_down))
        for r in range(k * PEERS // PIECES, (k + 1) * PEERS // PIECES):
            (back_keep if r == 0 else back_copies[r - 1]).start()

    rw = rw_ref[...]
    w0, w1 = rw[:, 0:1], rw[:, 1:2]
    place = iota((tok_rows, PLANE), 1)
    block, within = place // TILE, place % TILE
    dx, dy = jnp.zeros_like(place), jnp.zeros_like(place)
    for r, (rx, ry) in enumerate(OFFSETS):
        dx, dy = jnp.where(block == r, rx, dx), jnp.where(block == r, ry, dy)
    expert_of = ((x + dx) % 2) * 4 + (y + dy) % 4
    in0, in1 = id0 == expert_of, id1 == expert_of

    def weigh(slot):
        full = jnp.where(in0 & (slot0 == slot), w0, 0.0) + jnp.where(in1 & (slot1 == slot), w1, 0.0)
        high = full.astype(BF16).astype(F32)
        return jnp.concatenate([high, full - high], axis=0)

    weigh_main = weigh(within).astype(BF16)
    weigh_extra = weigh(TILE + within % EXTRA)
    group = jnp.concatenate([within // EXTRA] * 2, axis=0)

    back_keep.wait()
    for copy in back_copies:
        copy.wait_recv()
    for g in range(GROUPS):
        cols = slice(g * fold, (g + 1) * fold)
        both = jnp.dot(weigh_main, back_v[:, cols], preferred_element_type=F32)
        both += jnp.dot(jnp.where(group == g, weigh_extra, 0.0).astype(BF16), back_v[:, features:], preferred_element_type=F32)
        out_ref[:, cols] = (both[:tok_rows] + both[tok_rows:]).astype(BF16)

    for copy in (out_copies + twin_copies + up_copies + down_copies + on_up + on_down + to_above + to_below
                 + far_below + far_above + back_copies):
        copy.wait_send()


def shards(tokens, expert_ids, route_weights, up_weight, down_weight):
    tok_rows, features = tokens.shape
    units = up_weight.shape[1]
    width = features + features // GROUPS
    vmem = pl.BlockSpec(memory_space=pltpu.VMEM)
    anywhere = pl.BlockSpec(memory_space=pl.ANY)
    dma = pltpu.SemaphoreType.DMA
    return pl.pallas_call(
        kernel,
        out_shape=jax.ShapeDtypeStruct((tok_rows, features), BF16),
        in_specs=[vmem, vmem, vmem, anywhere, anywhere],
        out_specs=vmem,
        scratch_shapes=[
            pltpu.VMEM((2 * units, features), BF16),
            pltpu.VMEM((2 * units, features), BF16),
            pltpu.VMEM((4, ROWS, width), BF16),
            pltpu.VMEM((4, ROWS, width), BF16),
            pltpu.VMEM((PLANE, width), BF16),
            pltpu.VMEM((PLANE, width), BF16),
            pltpu.VMEM((PLANE, width), BF16),
            pltpu.VMEM((PLANE, width), BF16),
            pltpu.VMEM((8 * TILE, width), BF16),
            pltpu.VMEM((ROWS, 2 * units), BF16),
            pltpu.VMEM((PLANE, PLANE), BF16),
            pltpu.VMEM((PLANE, PLANE), BF16),
            dma((2,)), dma((2,)), dma((2,)), dma((2,)),
            dma((PEERS,)), dma((PEERS,)),
            dma((2, PIECES)), dma((2, PIECES)), dma((PIECES,)), dma((PIECES,)),
            dma((PIECES,)), dma((PIECES,)), dma((2, PIECES)), dma((2, PIECES)),
            dma((PEERS,)), dma((PEERS,)),
        ],
        compiler_params=pltpu.CompilerParams(
            collective_id=0, has_side_effects=True, vmem_limit_bytes=63 * 2**20),
        cost_estimate=pl.CostEstimate(
            flops=4 * 4 * ROWS * 2 * units * features, bytes_accessed=6 * units * features, transcendentals=0),
    )(tokens, expert_ids, route_weights, up_weight[0], down_weight[0])


def solution(mesh):
    return jax.shard_map(
        shards,
        mesh=mesh,
        in_specs=(
            P(("expert", "fsdp"), None),
            P(("expert", "fsdp"), None),
            P(("expert", "fsdp"), None),
            P("expert", "fsdp", None),
            P("expert", "fsdp", None),
        ),
        out_specs=P(("expert", "fsdp"), None),
        check_vma=False,
    )
```

```python
import jax
import jax.numpy as jnp
from jax import lax
from jax.experimental import pallas as pl
from jax.experimental.pallas import tpu as pltpu
from jax.sharding import PartitionSpec as P

MESH = pl.DeviceIdType.MESH
BF16, F32, I32 = jnp.bfloat16, jnp.float32, jnp.int32

OFFSETS = (
    (0, 0), (1, 1), (3, 3), (2, 2),
    (1, 3), (3, 1), (2, 0), (0, 2),
    (1, 2), (3, 2), (2, 1), (2, 3),
    (1, 0), (3, 0), (0, 1), (0, 3),
)
PEERS = len(OFFSETS)
BLOCKS = 8
TILE = 16
EXTRA = 2
GROUPS = TILE // EXTRA
PIECES = 4
PIECE = PEERS // PIECES * TILE
PLANE = PEERS * TILE
REST = PEERS * EXTRA
ROWS = PLANE + REST
TILE_N = 256
WAY_A, WAY_B = (0, 1), (2, 3)
FIRST_ROWS = (((0,), (0,)), ((), ()))
LAST_COLS = (((1,), (1,)), ((), ()))


def iota(shape, dim):
    return lax.broadcasted_iota(I32, shape, dim)


def onehot(mask):
    return jnp.where(mask, 1.0, 0.0).astype(BF16)


def kernel(
    tok_ref, meta_ref, up_ref, down_ref, out_ref,
    up_v, down_v, xp_v, xz_v, yp_v, yz_v, from_up, from_down, far_v, backp_v, backz_v, sendp_v, sendz_v,
    tok_v, meta_v, part_v, got_v, hid_v, perm_v, permt_v,
    sem_w, sem_ws, sem_wr, sem_self, sem_selfz, sem_ps, sem_pr, sem_as, sem_ar, sem_fs, sem_fr,
    sem_2s, sem_2r, sem_1s, sem_1r, sem_bs, sem_br,
    sem_ts, sem_tr, sem_ms, sem_mr, sem_zs, sem_zr, sem_ys, sem_yr, sem_gs, sem_gr,
):
    tok_rows, features = tok_ref.shape
    units = up_ref.shape[0]
    cols_z = tok_v.shape[2]
    cols_p = features - cols_z
    fold_p, fold_z = cols_p // GROUPS, cols_z // GROUPS
    e, f = lax.axis_index("expert"), lax.axis_index("fsdp")
    x_lo, y = e // 4, e % 4
    z, x_hi, core = f // 4, (f // 2) % 2, f % 2
    x = x_hi * 2 + x_lo

    def device(dx, dy, dz=0, dc=0):
        px, py, pz, pc = (x + dx) % 4, (y + dy) % 4, (z + dz) % 4, (core + dc) % 2
        return {"expert": (px % 2) * 4 + py, "fsdp": (pz * 2 + px // 2) * 2 + pc}

    peers = [device(dx, dy) for dx, dy in OFFSETS]
    backs = [device(-dx, -dy) for dx, dy in OFFSETS]
    planes = [None] + [device(0, 0, j) for j in (1, 2, 3)]
    above, below, twin = planes[1], planes[3], device(0, 0, 0, 1)

    barrier = pltpu.get_barrier_semaphore()
    greeted = peers[1:] + planes[1:] + [twin]
    for other in greeted:
        pl.semaphore_signal(barrier, inc=1, device_id=other, device_id_type=MESH)

    def link(src, dst, send, recv, to):
        return pltpu.make_async_remote_copy(
            src_ref=src, dst_ref=dst, send_sem=send, recv_sem=recv, device_id=to, device_id_type=MESH)

    own_up = pltpu.make_async_copy(up_ref, up_v.at[pl.ds(0, units)], sem_w.at[0])
    own_down = pltpu.make_async_copy(down_ref, down_v.at[pl.ds(0, units)], sem_w.at[1])
    own_up.start()
    own_down.start()

    lane_tok = iota((tok_rows, 2 * tok_rows), 1) % tok_rows
    earlier = onehot(iota((tok_rows, 2 * tok_rows), 0) < lane_tok)

    def slots_of(meta):
        id0, id1 = meta[0:1].astype(I32), meta[1:2].astype(I32)
        rows = iota((TILE, 2 * tok_rows), 0)
        is0, is1 = rows == id0, rows == id1
        chosen = onehot(is0 | is1)[:, :tok_rows]
        before = jnp.dot(chosen, earlier, preferred_element_type=F32)
        slot0 = jnp.sum(jnp.where(is0, before, 0.0), axis=0, keepdims=True).astype(I32)
        slot1 = jnp.sum(jnp.where(is1, before, 0.0), axis=0, keepdims=True).astype(I32)
        return id0, id1, slot0, slot1

    def picks_of(found):
        id0, id1, slot0, slot1 = [v[:, :tok_rows] for v in found]
        place = iota((BLOCKS * TILE, tok_rows), 0)
        block, within = place // TILE, place % TILE
        expert_of = ((x + block // 4) % 2) * 4 + (y + block % 4) % 4
        in0, in1 = id0 == expert_of, id1 == expert_of
        last = TILE + within % EXTRA
        main = onehot((in0 & (slot0 == within)) | (in1 & (slot1 == within)))
        rest = (in0 & (slot0 == last)) | (in1 & (slot1 == last))
        return main, [onehot(rest & (within // EXTRA == g)) for g in range(GROUPS)]

    def fill(dst, picks, src, first, cols):
        main, rest = picks
        fold = cols // GROUPS
        dst[:, 0:cols] = jnp.dot(main, src[:, first:first + cols], preferred_element_type=F32).astype(BF16)
        extra = jnp.zeros((BLOCKS * TILE, fold), F32)
        for g in range(GROUPS):
            extra += jnp.dot(rest[g], src[:, first + g * fold:first + (g + 1) * fold], preferred_element_type=F32)
        dst[:, cols:cols + fold] = extra.astype(BF16)

    own_slots = slots_of(meta_ref[...])
    own_picks = picks_of(own_slots)
    fill(sendp_v, own_picks, tok_ref, 0, cols_p)

    pl.semaphore_wait(barrier, len(greeted))

    tok_copies = [None] + [
        link(tok_ref.at[:, pl.ds(cols_p, cols_z)], tok_v.at[4 - j], sem_ts.at[j], sem_tr.at[4 - j], planes[j]) for j in (1, 2, 3)]
    meta_copies = [None] + [
        link(meta_ref, meta_v.at[4 - j], sem_ms.at[j], sem_mr.at[4 - j], planes[j]) for j in (1, 2, 3)]
    for j in (1, 3, 2):
        meta_copies[j].start()
        tok_copies[j].start()

    def from_block(r):
        dx, dy = OFFSETS[r]
        return pl.ds(((dx % 2) * 4 + dy) * TILE, TILE)

    def at_block(r):
        return pl.ds(r * TILE, TILE)

    keep = pltpu.make_async_copy(sendp_v.at[from_block(0)], xp_v.at[0, at_block(0)], sem_self.at[0])
    keep.start()
    out_copies = [
        link(sendp_v.at[from_block(r)], xp_v.at[0, at_block(r)], sem_ps.at[r], sem_pr.at[r], peers[r]) for r in range(1, PEERS)]
    for copy in out_copies:
        copy.start()

    keep_z = [pltpu.make_async_copy(sendz_v.at[j, from_block(0)], xz_v.at[j, at_block(0)], sem_selfz.at[0, j]) for j in range(4)]
    out_z = [
        [link(sendz_v.at[j, from_block(r)], xz_v.at[j, at_block(r)], sem_zs.at[j, r], sem_zr.at[j, r], peers[r])
         for r in range(1, PEERS)] for j in range(4)]

    def spread_z(j, picks, src, first):
        fill(sendz_v.at[j], picks, src, first, cols_z)
        keep_z[j].start()
        for copy in out_z[j]:
            copy.start()

    spread_z(0, own_picks, tok_ref, cols_p)

    twin_copies = [
        link(src, dst.at[pl.ds(units, units)], sem_ws.at[i], sem_wr.at[i], twin)
        for i, (src, dst) in enumerate(((up_ref, up_v), (down_ref, down_v)))]
    for copy in twin_copies:
        copy.start()

    out_row, in_row = iota((PLANE, PLANE), 0), iota((PLANE, PLANE), 1)
    perm_v[...] = onehot(in_row == (out_row % REST) // EXTRA * TILE + out_row // REST * EXTRA + out_row % EXTRA)
    permt_v[...] = onehot(out_row == (in_row % REST) // EXTRA * TILE + in_row // REST * EXTRA + in_row % EXTRA)

    def piece(k):
        return pl.ds(k * PIECE, PIECE)

    up_copies = [link(xp_v.at[0, piece(k)], xp_v.at[3, piece(k)], sem_as.at[0, k], sem_ar.at[0, k], above) for k in range(PIECES)]
    down_copies = [link(xp_v.at[0, piece(k)], xp_v.at[1, piece(k)], sem_as.at[1, k], sem_ar.at[1, k], below) for k in range(PIECES)]
    on_up = [link(xp_v.at[3, piece(k)], xp_v.at[2, piece(k)], sem_fs.at[k], sem_fr.at[k], above) for k in WAY_A]
    on_down = [link(xp_v.at[1, piece(k)], xp_v.at[2, piece(k)], sem_fs.at[k], sem_fr.at[k], below) for k in WAY_B]

    slots = [own_slots, None, None, None]
    for k in range(PIECES):
        for r in range(k * PEERS // PIECES, (k + 1) * PEERS // PIECES):
            if r == 0:
                keep.wait()
            else:
                out_copies[r - 1].wait_recv()
        up_copies[k].start()
        down_copies[k].start()
        if k < 3:
            j = (1, 3, 2)[k]
            meta_copies[4 - j].wait_recv()
            tok_copies[4 - j].wait_recv()
            slots[j] = slots_of(meta_v[j])
            spread_z(j, picks_of(slots[j]), tok_v.at[j], 0)

    parts = ((xp_v, yp_v, fold_p, cols_p), (xz_v, yz_v, fold_z, cols_z))

    def unfold(j):
        for x_v, _, fold, cols in parts:
            moved = jnp.dot(perm_v[...], x_v[j, 0:PLANE, cols:], preferred_element_type=F32).astype(BF16)
            for g in range(GROUPS):
                x_v[j, PLANE:ROWS, g * fold:(g + 1) * fold] = moved[g * REST:(g + 1) * REST]

    def refold(j, part):
        _, y_v, fold, cols = parts[part]
        total = jnp.zeros((PLANE, fold), F32)
        for g in range(GROUPS):
            total += jnp.dot(permt_v[:, g * REST:(g + 1) * REST], y_v[j, PLANE:ROWS, g * fold:(g + 1) * fold],
                             preferred_element_type=F32)
        y_v[j, 0:PLANE, cols:] = total.astype(BF16)

    def into_hidden(j, first, count):
        def body(n, carry):
            at = pl.ds(pl.multiple_of(n * TILE_N, TILE_N), TILE_N)
            v = lax.dot_general(xp_v[j, :, :cols_p], up_v[at, :cols_p], LAST_COLS, preferred_element_type=F32)
            v += lax.dot_general(xz_v[j, :, :cols_z], up_v[at, cols_p:], LAST_COLS, preferred_element_type=F32)
            hid_v[:, at] = (v / (1.0 + jnp.exp(-v))).astype(BF16)
            return carry

        lax.fori_loop(first // TILE_N, (first + count) // TILE_N, body, 0)

    def out_of_hidden(j, part):
        _, y_v, _, cols = parts[part]
        start = part * cols_p

        def body(n, carry):
            at = pl.ds(pl.multiple_of(n * TILE_N, TILE_N), TILE_N)
            down_at = pl.ds(pl.multiple_of(start + n * TILE_N, TILE_N), TILE_N)
            y_v[j, :, at] = jnp.dot(hid_v[...], down_v[:, down_at], preferred_element_type=F32).astype(BF16)
            return carry

        lax.fori_loop(0, cols // TILE_N, body, 0)
        refold(j, part)

    backz_keep = [pltpu.make_async_copy(yz_v.at[j, at_block(0)], backz_v.at[j, at_block(0)], sem_selfz.at[1, j]) for j in range(4)]
    backz_copies = [
        [link(yz_v.at[j, at_block(r)], backz_v.at[j, at_block(r)], sem_ys.at[j, r], sem_yr.at[j, r], backs[r])
         for r in range(1, PEERS)] for j in range(4)]

    def return_z(j):
        out_of_hidden(j, 1)
        backz_keep[j].start()
        for copy in backz_copies[j]:
            copy.start()

    def arrive_z(j):
        keep_z[j].wait()
        for copy in out_z[j]:
            copy.wait_recv()

    arrive_z(0)
    unfold(0)
    own_up.wait()
    into_hidden(0, 0, units)
    twin_copies[0].wait_recv()
    into_hidden(0, units, units)
    own_down.wait()
    twin_copies[1].wait_recv()
    return_z(0)
    out_of_hidden(0, 0)

    for i in range(len(WAY_A)):
        up_copies[WAY_A[i]].wait_recv()
        on_up[i].start()
    for k in range(PIECES):
        down_copies[k].wait_recv()
        if k in WAY_B:
            on_down[WAY_B.index(k)].start()
    for k in WAY_B:
        up_copies[k].wait_recv()

    to_above = [link(yp_v.at[1, piece(k)], from_down.at[piece(k)], sem_1s.at[0, k], sem_1r.at[0, k], above) for k in range(PIECES)]
    to_below = [link(yp_v.at[3, piece(k)], from_up.at[piece(k)], sem_1s.at[1, k], sem_1r.at[1, k], below) for k in range(PIECES)]
    far_below = [link(yp_v.at[2, piece(k)], far_v.at[piece(k)], sem_2s.at[k], sem_2r.at[k], below) for k in WAY_A]
    far_above = [link(yp_v.at[2, piece(k)], far_v.at[piece(k)], sem_2s.at[k], sem_2r.at[k], above) for k in WAY_B]

    def enter(j):
        arrive_z(j)
        unfold(j)
        into_hidden(j, 0, 2 * units)
        out_of_hidden(j, 0)

    enter(1)
    for k in WAY_A:
        to_above[k].start()
    return_z(1)
    enter(3)
    for k in WAY_B:
        to_below[k].start()
    return_z(3)
    for copy in on_up + on_down:
        copy.wait_recv()
    enter(2)
    for copy in far_below + far_above:
        copy.start()
    return_z(2)

    place = iota((PLANE, 2 * tok_rows), 0)
    block, within = place // TILE, place % TILE
    dx, dy = jnp.zeros_like(place), jnp.zeros_like(place)
    for r, (rx, ry) in enumerate(OFFSETS):
        dx, dy = jnp.where(block == r, rx, dx), jnp.where(block == r, ry, dy)
    expert_of = ((x + dx) % 2) * 4 + (y + dy) % 4
    is_high = iota((PLANE, 2 * tok_rows), 1) < tok_rows

    def weigh(found, meta, slot):
        id0, id1, slot0, slot1 = found
        full = (jnp.where((id0 == expert_of) & (slot0 == slot), meta[2:3], 0.0)
                + jnp.where((id1 == expert_of) & (slot1 == slot), meta[3:4], 0.0))
        high = full.astype(BF16).astype(F32)
        return jnp.where(is_high, high, full - high)

    def combine(found, meta, src, cols, put):
        fold = cols // GROUPS
        main = weigh(found, meta, within).astype(BF16)
        rest = weigh(found, meta, TILE + within % EXTRA)
        for g in range(GROUPS):
            at = slice(g * fold, (g + 1) * fold)
            both = lax.dot_general(main, src[:, at], FIRST_ROWS, preferred_element_type=F32)
            both += lax.dot_general(jnp.where(within // EXTRA == g, rest, 0.0).astype(BF16), src[:, cols:],
                                    FIRST_ROWS, preferred_element_type=F32)
            put(at, both[:tok_rows] + both[tok_rows:])

    part_copies = [None] + [link(part_v.at[j], got_v.at[j], sem_gs.at[j], sem_gr.at[j], planes[j]) for j in (1, 2, 3)]

    def gather_z(j):
        backz_keep[j].wait()
        for copy in backz_copies[j]:
            copy.wait_recv()

        def put(at, value):
            part_v[j, :, at] = value.astype(BF16)

        combine(slots[j], meta_ref[...] if j == 0 else meta_v[j], backz_v.at[j], cols_z, put)
        if j:
            part_copies[j].start()

    gather_z(0)
    gather_z(1)

    def add_into(target, j, k, others):
        total = target[j, piece(k), :].astype(F32)
        for other in others:
            total += other[piece(k), :].astype(F32)
        target[j, piece(k), :] = total.astype(BF16)

    for i in range(len(WAY_A)):
        far_below[i].wait_recv()
        add_into(yp_v, 3, WAY_A[i], (far_v,))
        to_below[WAY_A[i]].start()
        far_above[i].wait_recv()
        add_into(yp_v, 1, WAY_B[i], (far_v,))
        to_above[WAY_B[i]].start()

    gather_z(3)
    gather_z(2)

    back_keep = pltpu.make_async_copy(yp_v.at[0, at_block(0)], backp_v.at[at_block(0)], sem_self.at[1])
    back_copies = [
        link(yp_v.at[0, at_block(r)], backp_v.at[at_block(r)], sem_bs.at[r], sem_br.at[r], backs[r]) for r in range(1, PEERS)]
    for k in (0, 2, 1, 3):
        to_above[k].wait_recv()
        to_below[k].wait_recv()
        add_into(yp_v, 0, k, (from_up, from_down))
        for r in range(k * PEERS // PIECES, (k + 1) * PEERS // PIECES):
            (back_keep if r == 0 else back_copies[r - 1]).start()

    for j in (1, 2, 3):
        part_copies[j].wait_recv()
    total = part_v[0].astype(F32)
    for j in (1, 2, 3):
        total += got_v[j].astype(F32)
    out_ref[:, cols_p:] = total.astype(BF16)

    back_keep.wait()
    for copy in back_copies:
        copy.wait_recv()

    def put_out(at, value):
        out_ref[:, at] = value.astype(BF16)

    combine(own_slots, meta_ref[...], backp_v, cols_p, put_out)

    for copy in (out_copies + twin_copies + up_copies + down_copies + on_up + on_down + to_above + to_below
                 + far_below + far_above + back_copies + tok_copies[1:] + meta_copies[1:] + part_copies[1:]):
        copy.wait_send()
    for j in range(4):
        for copy in out_z[j] + backz_copies[j]:
            copy.wait_send()


def shards(tokens, expert_ids, route_weights, up_weight, down_weight):
    tok_rows, features = tokens.shape
    units = up_weight.shape[1]
    cols_z = features // 3
    cols_p = features - cols_z
    wide_p, wide_z = cols_p + cols_p // GROUPS, cols_z + cols_z // GROUPS
    meta = jnp.concatenate([expert_ids.T.astype(F32), route_weights.T, jnp.zeros((4, tok_rows), F32)], axis=0)
    meta = jnp.concatenate([meta, meta], axis=1)
    vmem = pl.BlockSpec(memory_space=pltpu.VMEM)
    anywhere = pl.BlockSpec(memory_space=pl.ANY)
    dma = pltpu.SemaphoreType.DMA
    return pl.pallas_call(
        kernel,
        out_shape=jax.ShapeDtypeStruct((tok_rows, features), BF16),
        in_specs=[vmem, vmem, anywhere, anywhere],
        out_specs=vmem,
        scratch_shapes=[
            pltpu.VMEM((2 * units, features), BF16),
            pltpu.VMEM((2 * units, features), BF16),
            pltpu.VMEM((4, ROWS, wide_p), BF16),
            pltpu.VMEM((4, ROWS, wide_z), BF16),
            pltpu.VMEM((4, ROWS, wide_p), BF16),
            pltpu.VMEM((4, ROWS, wide_z), BF16),
            pltpu.VMEM((PLANE, wide_p), BF16),
            pltpu.VMEM((PLANE, wide_p), BF16),
            pltpu.VMEM((PLANE, wide_p), BF16),
            pltpu.VMEM((PLANE, wide_p), BF16),
            pltpu.VMEM((4, PLANE, wide_z), BF16),
            pltpu.VMEM((BLOCKS * TILE, wide_p), BF16),
            pltpu.VMEM((4, BLOCKS * TILE, wide_z), BF16),
            pltpu.VMEM((4, tok_rows, cols_z), BF16),
            pltpu.VMEM((4, 8, 2 * tok_rows), F32),
            pltpu.VMEM((4, tok_rows, cols_z), BF16),
            pltpu.VMEM((4, tok_rows, cols_z), BF16),
            pltpu.VMEM((ROWS, 2 * units), BF16),
            pltpu.VMEM((PLANE, PLANE), BF16),
            pltpu.VMEM((PLANE, PLANE), BF16),
            dma((2,)), dma((2,)), dma((2,)), dma((2,)), dma((2, 4)),
            dma((PEERS,)), dma((PEERS,)),
            dma((2, PIECES)), dma((2, PIECES)), dma((PIECES,)), dma((PIECES,)),
            dma((PIECES,)), dma((PIECES,)), dma((2, PIECES)), dma((2, PIECES)),
            dma((PEERS,)), dma((PEERS,)),
            dma((4,)), dma((4,)), dma((4,)), dma((4,)),
            dma((4, PEERS)), dma((4, PEERS)), dma((4, PEERS)), dma((4, PEERS)), dma((4,)), dma((4,)),
        ],
        compiler_params=pltpu.CompilerParams(
            collective_id=0, has_side_effects=True, vmem_limit_bytes=63 * 2**20),
        cost_estimate=pl.CostEstimate(
            flops=4 * 4 * ROWS * 2 * units * features, bytes_accessed=6 * units * features, transcendentals=0),
    )(tokens, meta, up_weight[0], down_weight[0])


def solution(mesh):
    return jax.shard_map(
        shards,
        mesh=mesh,
        in_specs=(
            P(("expert", "fsdp"), None),
            P(("expert", "fsdp"), None),
            P(("expert", "fsdp"), None),
            P("expert", "fsdp", None),
            P("expert", "fsdp", None),
        ),
        out_specs=P(("expert", "fsdp"), None),
        check_vma=False,
    )
```

```python
import jax
import jax.numpy as jnp
from jax import lax
from jax.experimental import pallas as pl
from jax.experimental.pallas import tpu as pltpu
from jax.sharding import PartitionSpec as P

MESH = pl.DeviceIdType.MESH
BF16, F32, I32 = jnp.bfloat16, jnp.float32, jnp.int32

OFFSETS = (
    (0, 0), (1, 1), (3, 3), (2, 2),
    (1, 2), (3, 2), (2, 1), (2, 3),
    (1, 3), (3, 1), (2, 0), (0, 2),
    (1, 0), (3, 0), (0, 1), (0, 3),
)
PIECE_ORDER = (0, 2, 1, 3)
PEERS = len(OFFSETS)
BLOCKS = 8
TILE = 16
EXTRA = 2
GROUPS = TILE // EXTRA
PIECES = 4
PIECE = PEERS // PIECES * TILE
PLANE = PEERS * TILE
REST = PEERS * EXTRA
ROWS = PLANE + REST
TILE_N = 1024
WAY_A, WAY_B = (0, 1), (2, 3)
FIRST_ROWS = (((0,), (0,)), ((), ()))
LAST_COLS = (((1,), (1,)), ((), ()))


def batch_of(j, k):
    return j if j % 2 == 0 or k in WAY_A else 4 - j


def pairs_of(batch):
    return [(j, k) for j in range(4) for k in range(PIECES) if batch_of(j, k) == batch]


def offsets_of(k):
    return range(k * PEERS // PIECES, (k + 1) * PEERS // PIECES)


def iota(shape, dim):
    return lax.broadcasted_iota(I32, shape, dim)


def onehot(mask):
    return jnp.where(mask, 1.0, 0.0).astype(BF16)


def kernel(
    tok_ref, ids_ref, rw_ref, up_ref, down_ref, out_ref,
    up_v, down_v, xp_v, xz_v, yp_v, yz_v, from_up, from_down, far_v, backp_v, backz_v, sendp_v, sendz_v,
    tok_v, meta_v, part_v, got_v, hid_v, perm_v, permt_v,
    sem_w, sem_ws, sem_wr, sem_self, sem_selfz, sem_ps, sem_pr, sem_as, sem_ar, sem_fs, sem_fr,
    sem_2s, sem_2r, sem_1s, sem_1r, sem_bs, sem_br,
    sem_ts, sem_tr, sem_ms, sem_mr, sem_zs, sem_zr, sem_ys, sem_yr, sem_gs, sem_gr,
):
    tok_rows, features = tok_ref.shape
    units = up_ref.shape[0]
    cols_z = tok_v.shape[2]
    cols_p = features - cols_z
    fold_p, fold_z = cols_p // GROUPS, cols_z // GROUPS
    e, f = lax.axis_index("expert"), lax.axis_index("fsdp")
    x_lo, y = e // 4, e % 4
    z, x_hi, core = f // 4, (f // 2) % 2, f % 2
    x = x_hi * 2 + x_lo

    def device(dx, dy, dz=0, dc=0):
        px, py, pz, pc = (x + dx) % 4, (y + dy) % 4, (z + dz) % 4, (core + dc) % 2
        return {"expert": (px % 2) * 4 + py, "fsdp": (pz * 2 + px // 2) * 2 + pc}

    peers = [device(dx, dy) for dx, dy in OFFSETS]
    backs = [device(-dx, -dy) for dx, dy in OFFSETS]
    planes = [None] + [device(0, 0, j) for j in (1, 2, 3)]
    above, below, twin = planes[1], planes[3], device(0, 0, 0, 1)

    barrier = pltpu.get_barrier_semaphore()
    greeted = peers[1:] + planes[1:] + [twin]
    for other in greeted:
        pl.semaphore_signal(barrier, inc=1, device_id=other, device_id_type=MESH)

    def link(src, dst, send, recv, to):
        return pltpu.make_async_remote_copy(
            src_ref=src, dst_ref=dst, send_sem=send, recv_sem=recv, device_id=to, device_id_type=MESH)

    own_up = pltpu.make_async_copy(up_ref, up_v.at[pl.ds(0, units)], sem_w.at[0])
    own_down = pltpu.make_async_copy(down_ref, down_v.at[pl.ds(0, units)], sem_w.at[1])
    own_up.start()
    own_down.start()

    lane_tok = iota((tok_rows, 2 * tok_rows), 1) % tok_rows
    earlier = onehot(iota((tok_rows, 2 * tok_rows), 0) < lane_tok)

    def slots_of(meta):
        id0, id1 = meta[0:1].astype(I32), meta[1:2].astype(I32)
        rows = iota((TILE, 2 * tok_rows), 0)
        is0, is1 = rows == id0, rows == id1
        chosen = onehot(is0 | is1)[:, :tok_rows]
        before = jnp.dot(chosen, earlier, preferred_element_type=F32)
        slot0 = jnp.sum(jnp.where(is0, before, 0.0), axis=0, keepdims=True).astype(I32)
        slot1 = jnp.sum(jnp.where(is1, before, 0.0), axis=0, keepdims=True).astype(I32)
        return id0, id1, slot0, slot1

    def picks_of(found):
        id0, id1, slot0, slot1 = [v[:, :tok_rows] for v in found]
        place = iota((BLOCKS * TILE, tok_rows), 0)
        block, within = place // TILE, place % TILE
        expert_of = ((x + block // 4) % 2) * 4 + (y + block % 4) % 4
        in0, in1 = id0 == expert_of, id1 == expert_of
        last = TILE + within % EXTRA
        main = onehot((in0 & (slot0 == within)) | (in1 & (slot1 == within)))
        rest = (in0 & (slot0 == last)) | (in1 & (slot1 == last))
        return main, [onehot(rest & (within // EXTRA == g)) for g in range(GROUPS)]

    def fill(dst, picks, src, first, cols):
        main, rest = picks
        fold = cols // GROUPS
        dst[:, 0:cols] = jnp.dot(main, src[:, first:first + cols], preferred_element_type=F32).astype(BF16)
        extra = jnp.zeros((BLOCKS * TILE, fold), F32)
        for g in range(GROUPS):
            extra += jnp.dot(rest[g], src[:, first + g * fold:first + (g + 1) * fold], preferred_element_type=F32)
        dst[:, cols:cols + fold] = extra.astype(BF16)

    meta_ref = meta_v.at[0]
    meta_v[0] = jnp.zeros((8, 2 * tok_rows), F32)
    for at in (slice(0, tok_rows), slice(tok_rows, 2 * tok_rows)):
        meta_v[0, 0:2, at] = ids_ref[...].astype(F32)
        meta_v[0, 2:4, at] = rw_ref[...]
    own_slots = slots_of(meta_ref[...])
    own_picks = picks_of(own_slots)
    fill(sendp_v, own_picks, tok_ref, 0, cols_p)

    pl.semaphore_wait(barrier, len(greeted))

    tok_copies = [None] + [
        link(tok_ref.at[:, pl.ds(cols_p, cols_z)], tok_v.at[4 - j], sem_ts.at[j], sem_tr.at[4 - j], planes[j]) for j in (1, 2, 3)]
    meta_copies = [None] + [
        link(meta_ref, meta_v.at[4 - j], sem_ms.at[j], sem_mr.at[4 - j], planes[j]) for j in (1, 2, 3)]
    for j in (1, 3, 2):
        meta_copies[j].start()
        tok_copies[j].start()

    def from_block(r):
        dx, dy = OFFSETS[r]
        return pl.ds(((dx % 2) * 4 + dy) * TILE, TILE)

    def at_block(r):
        return pl.ds(r * TILE, TILE)

    keep = pltpu.make_async_copy(sendp_v.at[from_block(0)], xp_v.at[0, at_block(0)], sem_self.at[0])
    keep.start()
    out_copies = [
        link(sendp_v.at[from_block(r)], xp_v.at[0, at_block(r)], sem_ps.at[r], sem_pr.at[r], peers[r]) for r in range(1, PEERS)]
    for k in PIECE_ORDER:
        for r in offsets_of(k):
            if r:
                out_copies[r - 1].start()

    keep_z = [pltpu.make_async_copy(sendz_v.at[j, from_block(0)], xz_v.at[batch_of(j, 0), at_block(0)], sem_selfz.at[0, j]) for j in range(4)]
    out_z = [
        [link(sendz_v.at[j, from_block(r)], xz_v.at[batch_of(j, r * PIECES // PEERS), at_block(r)], sem_zs.at[j, r], sem_zr.at[j, r], peers[r])
         for r in range(1, PEERS)] for j in range(4)]

    def spread_z(j, picks, src, first):
        fill(sendz_v.at[j], picks, src, first, cols_z)
        for k in PIECE_ORDER:
            for r in offsets_of(k):
                (out_z[j][r - 1] if r else keep_z[j]).start()

    twin_copies = [
        link(src, dst.at[pl.ds(units, units)], sem_ws.at[i], sem_wr.at[i], twin)
        for i, (src, dst) in enumerate(((up_ref, up_v), (down_ref, down_v)))]
    for copy in twin_copies:
        copy.start()

    out_row, in_row = iota((PLANE, PLANE), 0), iota((PLANE, PLANE), 1)
    perm_v[...] = onehot(in_row == (out_row % REST) // EXTRA * TILE + out_row // REST * EXTRA + out_row % EXTRA)
    permt_v[...] = onehot(out_row == (in_row % REST) // EXTRA * TILE + in_row // REST * EXTRA + in_row % EXTRA)

    def piece(k):
        return pl.ds(k * PIECE, PIECE)

    def xp_at(j, k):
        return xp_v.at[batch_of(j, k), piece(k)]

    def yp_at(j, k):
        return yp_v.at[batch_of(j, k), piece(k)]

    up_copies = [link(xp_at(0, k), xp_at(3, k), sem_as.at[0, k], sem_ar.at[0, k], above) for k in range(PIECES)]
    down_copies = [link(xp_at(0, k), xp_at(1, k), sem_as.at[1, k], sem_ar.at[1, k], below) for k in range(PIECES)]
    on_down = {k: link(xp_at(1, k), xp_at(2, k), sem_fs.at[k], sem_fr.at[k], below) for k in WAY_A}
    on_up = {k: link(xp_at(3, k), xp_at(2, k), sem_fs.at[k], sem_fr.at[k], above) for k in WAY_B}

    slots = [own_slots, None, None, None]
    for k, j in zip(PIECE_ORDER, (1, 3, 0, 2)):
        if j:
            meta_copies[4 - j].wait_recv()
            tok_copies[4 - j].wait_recv()
            slots[j] = slots_of(meta_v[j])
            spread_z(j, picks_of(slots[j]), tok_v.at[j], 0)
        else:
            spread_z(0, own_picks, tok_ref, cols_p)
        for r in offsets_of(k):
            if r == 0:
                keep.wait()
            else:
                out_copies[r - 1].wait_recv()
        (down_copies if k in WAY_A else up_copies)[k].start()
    for a, b in zip(WAY_A, WAY_B):
        down_copies[b].start()
        up_copies[a].start()

    parts = ((xp_v, yp_v, fold_p, cols_p), (xz_v, yz_v, fold_z, cols_z))

    def unfold(j):
        for x_v, _, fold, cols in parts:
            moved = jnp.dot(perm_v[...], x_v[j, 0:PLANE, cols:], preferred_element_type=F32).astype(BF16)
            for g in range(GROUPS):
                x_v[j, PLANE:ROWS, g * fold:(g + 1) * fold] = moved[g * REST:(g + 1) * REST]

    def refold(j, part):
        _, y_v, fold, cols = parts[part]
        total = jnp.zeros((PLANE, fold), F32)
        for g in range(GROUPS):
            total += jnp.dot(permt_v[:, g * REST:(g + 1) * REST], y_v[j, PLANE:ROWS, g * fold:(g + 1) * fold],
                             preferred_element_type=F32)
        y_v[j, 0:PLANE, cols:] = total.astype(BF16)

    def into_hidden(j):
        def body(n, carry):
            at = pl.ds(pl.multiple_of(n * TILE_N, TILE_N), TILE_N)
            v = lax.dot_general(xp_v[j, :, :cols_p], up_v[at, :cols_p], LAST_COLS, preferred_element_type=F32)
            v += lax.dot_general(xz_v[j, :, :cols_z], up_v[at, cols_p:], LAST_COLS, preferred_element_type=F32)
            hid_v[:, at] = (v / (1.0 + jnp.exp(-v))).astype(BF16)
            return carry

        lax.fori_loop(0, 2 * units // TILE_N, body, 0)

    def out_of_hidden(j, part):
        _, y_v, _, cols = parts[part]
        start = part * cols_p

        def body(n, carry):
            at = pl.ds(pl.multiple_of(n * TILE_N, TILE_N), TILE_N)
            down_at = pl.ds(pl.multiple_of(start + n * TILE_N, TILE_N), TILE_N)
            y_v[j, :, at] = jnp.dot(hid_v[...], down_v[:, down_at], preferred_element_type=F32).astype(BF16)
            return carry

        lax.fori_loop(0, cols // TILE_N, body, 0)
        refold(j, part)

    backz_keep = [pltpu.make_async_copy(yz_v.at[batch_of(j, 0), at_block(0)], backz_v.at[j, at_block(0)], sem_selfz.at[1, j]) for j in range(4)]
    backz_copies = [
        [link(yz_v.at[batch_of(j, r * PIECES // PEERS), at_block(r)], backz_v.at[j, at_block(r)], sem_ys.at[j, r], sem_yr.at[j, r], backs[r])
         for r in range(1, PEERS)] for j in range(4)]

    def return_z(batch):
        out_of_hidden(batch, 1)
        for j, k in pairs_of(batch):
            for r in offsets_of(k):
                (backz_copies[j][r - 1] if r else backz_keep[j]).start()

    def enter(batch):
        for j, k in pairs_of(batch):
            for r in offsets_of(k):
                if r:
                    out_z[j][r - 1].wait_recv()
                else:
                    keep_z[j].wait()
        unfold(batch)
        into_hidden(batch)
        out_of_hidden(batch, 0)

    to_above = [link(yp_at(1, k), from_down.at[piece(k)], sem_1s.at[0, k], sem_1r.at[0, k], above) for k in range(PIECES)]
    to_below = [link(yp_at(3, k), from_up.at[piece(k)], sem_1s.at[1, k], sem_1r.at[1, k], below) for k in range(PIECES)]
    far_below = {k: link(yp_at(2, k), far_v.at[piece(k)], sem_2s.at[k], sem_2r.at[k], below) for k in WAY_A}
    far_above = {k: link(yp_at(2, k), far_v.at[piece(k)], sem_2s.at[k], sem_2r.at[k], above) for k in WAY_B}

    for a, b in zip(WAY_A, WAY_B):
        down_copies[a].wait_recv()
        on_down[a].start()
        up_copies[b].wait_recv()
        on_up[b].start()
    own_up.wait()
    twin_copies[0].wait_recv()
    own_down.wait()
    twin_copies[1].wait_recv()
    enter(1)
    for a, b in zip(WAY_A, WAY_B):
        to_above[a].start()
        to_below[b].start()
    return_z(1)
    for a, b in zip(WAY_A, WAY_B):
        down_copies[b].wait_recv()
        up_copies[a].wait_recv()
    enter(3)
    return_z(3)
    for a, b in zip(WAY_A, WAY_B):
        on_down[a].wait_recv()
        on_up[b].wait_recv()
    enter(2)
    for a, b in zip(WAY_A, WAY_B):
        far_below[a].start()
        far_above[b].start()
    return_z(2)

    place = iota((PLANE, 2 * tok_rows), 0)
    block, within = place // TILE, place % TILE
    dx, dy = jnp.zeros_like(place), jnp.zeros_like(place)
    for r, (rx, ry) in enumerate(OFFSETS):
        dx, dy = jnp.where(block == r, rx, dx), jnp.where(block == r, ry, dy)
    expert_of = ((x + dx) % 2) * 4 + (y + dy) % 4
    is_high = iota((PLANE, 2 * tok_rows), 1) < tok_rows

    def weigh(found, meta, slot):
        id0, id1, slot0, slot1 = found
        full = (jnp.where((id0 == expert_of) & (slot0 == slot), meta[2:3], 0.0)
                + jnp.where((id1 == expert_of) & (slot1 == slot), meta[3:4], 0.0))
        high = full.astype(BF16).astype(F32)
        return jnp.where(is_high, high, full - high)

    def combine(found, meta, src, cols, put):
        fold = cols // GROUPS
        main = weigh(found, meta, within).astype(BF16)
        rest = weigh(found, meta, TILE + within % EXTRA)
        for g in range(GROUPS):
            at = slice(g * fold, (g + 1) * fold)
            both = lax.dot_general(main, src[:, at], FIRST_ROWS, preferred_element_type=F32)
            both += lax.dot_general(jnp.where(within // EXTRA == g, rest, 0.0).astype(BF16), src[:, cols:],
                                    FIRST_ROWS, preferred_element_type=F32)
            put(at, both[:tok_rows] + both[tok_rows:])

    part_copies = [None] + [link(part_v.at[j], got_v.at[j], sem_gs.at[j], sem_gr.at[j], planes[j]) for j in (1, 2, 3)]

    def gather_z(j):
        backz_keep[j].wait()
        for copy in backz_copies[j]:
            copy.wait_recv()

        def put(at, value):
            part_v[j, :, at] = value.astype(BF16)

        combine(slots[j], meta_ref[...] if j == 0 else meta_v[j], backz_v.at[j], cols_z, put)
        if j:
            part_copies[j].start()

    gather_z(1)
    enter(0)
    return_z(0)

    def add_into(target, j, k, others):
        total = target[j, piece(k), :].astype(F32)
        for other in others:
            total += other[piece(k), :].astype(F32)
        target[j, piece(k), :] = total.astype(BF16)

    for a, b, j in zip(WAY_A, WAY_B, (3, 2)):
        far_below[a].wait_recv()
        add_into(yp_v, 3, a, (far_v,))
        to_below[a].start()
        far_above[b].wait_recv()
        add_into(yp_v, 3, b, (far_v,))
        to_above[b].start()
        gather_z(j)
    gather_z(0)

    back_keep = pltpu.make_async_copy(yp_v.at[0, at_block(0)], backp_v.at[at_block(0)], sem_self.at[1])
    back_copies = [
        link(yp_v.at[0, at_block(r)], backp_v.at[at_block(r)], sem_bs.at[r], sem_br.at[r], backs[r]) for r in range(1, PEERS)]
    for k in PIECE_ORDER:
        to_above[k].wait_recv()
        to_below[k].wait_recv()
        add_into(yp_v, 0, k, (from_up, from_down))
        for r in offsets_of(k):
            (back_keep if r == 0 else back_copies[r - 1]).start()

    for j in (1, 2, 3):
        part_copies[j].wait_recv()
    total = part_v[0].astype(F32)
    for j in (1, 2, 3):
        total += got_v[j].astype(F32)
    out_ref[:, cols_p:] = total.astype(BF16)

    back_keep.wait()
    for copy in back_copies:
        copy.wait_recv()

    def put_out(at, value):
        out_ref[:, at] = value.astype(BF16)

    combine(own_slots, meta_ref[...], backp_v, cols_p, put_out)

    onward = [way[k] for way in (on_up, on_down, far_below, far_above) for k in sorted(way)]
    for copy in (out_copies + twin_copies + up_copies + down_copies + to_above + to_below + onward + back_copies + tok_copies[1:] + meta_copies[1:] + part_copies[1:]):
        copy.wait_send()
    for j in range(4):
        for copy in out_z[j] + backz_copies[j]:
            copy.wait_send()


def shards(tokens, expert_ids, route_weights, up_weight, down_weight):
    tok_rows, features = tokens.shape
    units = up_weight.shape[1]
    cols_z = features // 3
    cols_p = features - cols_z
    wide_p, wide_z = cols_p + cols_p // GROUPS, cols_z + cols_z // GROUPS
    vmem = pl.BlockSpec(memory_space=pltpu.VMEM)
    anywhere = pl.BlockSpec(memory_space=pl.ANY)
    dma = pltpu.SemaphoreType.DMA
    return pl.pallas_call(
        kernel,
        out_shape=jax.ShapeDtypeStruct((tok_rows, features), BF16),
        in_specs=[vmem, vmem, vmem, anywhere, anywhere],
        out_specs=vmem,
        scratch_shapes=[
            pltpu.VMEM((2 * units, features), BF16),
            pltpu.VMEM((2 * units, features), BF16),
            pltpu.VMEM((4, ROWS, wide_p), BF16),
            pltpu.VMEM((4, ROWS, wide_z), BF16),
            pltpu.VMEM((4, ROWS, wide_p), BF16),
            pltpu.VMEM((4, ROWS, wide_z), BF16),
            pltpu.VMEM((PLANE, wide_p), BF16),
            pltpu.VMEM((PLANE, wide_p), BF16),
            pltpu.VMEM((PLANE, wide_p), BF16),
            pltpu.VMEM((PLANE, wide_p), BF16),
            pltpu.VMEM((4, PLANE, wide_z), BF16),
            pltpu.VMEM((BLOCKS * TILE, wide_p), BF16),
            pltpu.VMEM((4, BLOCKS * TILE, wide_z), BF16),
            pltpu.VMEM((4, tok_rows, cols_z), BF16),
            pltpu.VMEM((4, 8, 2 * tok_rows), F32),
            pltpu.VMEM((4, tok_rows, cols_z), BF16),
            pltpu.VMEM((4, tok_rows, cols_z), BF16),
            pltpu.VMEM((ROWS, 2 * units), BF16),
            pltpu.VMEM((PLANE, PLANE), BF16),
            pltpu.VMEM((PLANE, PLANE), BF16),
            dma((2,)), dma((2,)), dma((2,)), dma((2,)), dma((2, 4)),
            dma((PEERS,)), dma((PEERS,)),
            dma((2, PIECES)), dma((2, PIECES)), dma((PIECES,)), dma((PIECES,)),
            dma((PIECES,)), dma((PIECES,)), dma((2, PIECES)), dma((2, PIECES)),
            dma((PEERS,)), dma((PEERS,)),
            dma((4,)), dma((4,)), dma((4,)), dma((4,)),
            dma((4, PEERS)), dma((4, PEERS)), dma((4, PEERS)), dma((4, PEERS)), dma((4,)), dma((4,)),
        ],
        compiler_params=pltpu.CompilerParams(
            collective_id=0, has_side_effects=True, vmem_limit_bytes=63 * 2**20),
        cost_estimate=pl.CostEstimate(
            flops=4 * 4 * ROWS * 2 * units * features, bytes_accessed=6 * units * features, transcendentals=0),
    )(tokens, expert_ids.T, route_weights.T, up_weight[0], down_weight[0])


def solution(mesh):
    return jax.shard_map(
        shards,
        mesh=mesh,
        in_specs=(
            P(("expert", "fsdp"), None),
            P(("expert", "fsdp"), None),
            P(("expert", "fsdp"), None),
            P("expert", "fsdp", None),
            P("expert", "fsdp", None),
        ),
        out_specs=P(("expert", "fsdp"), None),
        check_vma=False,
    )
```

```python
import jax
import jax.numpy as jnp
from jax import lax
from jax.experimental import pallas as pl
from jax.experimental.pallas import tpu as pltpu
from jax.sharding import PartitionSpec as P

MESH = pl.DeviceIdType.MESH
BF16, F32, I32 = jnp.bfloat16, jnp.float32, jnp.int32

OFFSETS = (
    (0, 0), (1, 1), (3, 3), (2, 2),
    (1, 2), (3, 2), (2, 1), (2, 3),
    (1, 3), (3, 1), (2, 0), (0, 2),
    (1, 0), (3, 0), (0, 1), (0, 3),
)
PIECE_ORDER = (0, 4, 1, 5, 2, 6, 3, 7)
PEERS = len(OFFSETS)
BLOCKS = 8
TILE = 16
EXTRA = 2
GROUPS = TILE // EXTRA
PIECES = 8
PIECE = PEERS // PIECES * TILE
PLANE = PEERS * TILE
REST = PEERS * EXTRA
ROWS = PLANE + REST
TILE_N = 1024
WAY_A, WAY_B = (0, 1, 2, 3), (4, 5, 6, 7)
FIRST_ROWS = (((0,), (0,)), ((), ()))
LAST_COLS = (((1,), (1,)), ((), ()))


def batch_of(j, k):
    return j if j % 2 == 0 or k in WAY_A else 4 - j


def pairs_of(batch):
    return [(j, k) for j in range(4) for k in range(PIECES) if batch_of(j, k) == batch]


def offsets_of(k):
    return range(k * PEERS // PIECES, (k + 1) * PEERS // PIECES)


def iota(shape, dim):
    return lax.broadcasted_iota(I32, shape, dim)


def onehot(mask):
    return jnp.where(mask, 1.0, 0.0).astype(BF16)


def kernel(
    tok_ref, ids_ref, rw_ref, up_ref, down_ref, out_ref,
    up_v, down_v, xp_v, xz_v, yp_v, yz_v, from_up, from_down, far_v, backp_v, backz_v, sendp_v, sendz_v,
    tok_v, meta_v, part_v, got_v, hid_v, perm_v, permt_v,
    sem_w, sem_ws, sem_wr, sem_self, sem_selfz, sem_ps, sem_pr, sem_as, sem_ar, sem_fs, sem_fr,
    sem_2s, sem_2r, sem_1s, sem_1r, sem_bs, sem_br,
    sem_ts, sem_tr, sem_ms, sem_mr, sem_zs, sem_zr, sem_ys, sem_yr, sem_gs, sem_gr,
):
    tok_rows, features = tok_ref.shape
    units = up_ref.shape[0]
    cols_z = tok_v.shape[2]
    cols_p = features - cols_z
    fold_p, fold_z = cols_p // GROUPS, cols_z // GROUPS
    e, f = lax.axis_index("expert"), lax.axis_index("fsdp")
    x_lo, y = e // 4, e % 4
    z, x_hi, core = f // 4, (f // 2) % 2, f % 2
    x = x_hi * 2 + x_lo

    def device(dx, dy, dz=0, dc=0):
        px, py, pz, pc = (x + dx) % 4, (y + dy) % 4, (z + dz) % 4, (core + dc) % 2
        return {"expert": (px % 2) * 4 + py, "fsdp": (pz * 2 + px // 2) * 2 + pc}

    peers = [device(dx, dy) for dx, dy in OFFSETS]
    backs = [device(-dx, -dy) for dx, dy in OFFSETS]
    planes = [None] + [device(0, 0, j) for j in (1, 2, 3)]
    above, below, twin = planes[1], planes[3], device(0, 0, 0, 1)

    barrier = pltpu.get_barrier_semaphore()
    greeted = peers[1:] + planes[1:] + [twin]
    for other in greeted:
        pl.semaphore_signal(barrier, inc=1, device_id=other, device_id_type=MESH)

    def link(src, dst, send, recv, to):
        return pltpu.make_async_remote_copy(
            src_ref=src, dst_ref=dst, send_sem=send, recv_sem=recv, device_id=to, device_id_type=MESH)

    own_up = pltpu.make_async_copy(up_ref, up_v.at[pl.ds(0, units)], sem_w.at[0])
    own_down = pltpu.make_async_copy(down_ref, down_v.at[pl.ds(0, units)], sem_w.at[1])
    own_up.start()
    own_down.start()

    lane_tok = iota((tok_rows, 2 * tok_rows), 1) % tok_rows
    earlier = onehot(iota((tok_rows, 2 * tok_rows), 0) < lane_tok)

    def slots_of(meta):
        id0, id1 = meta[0:1].astype(I32), meta[1:2].astype(I32)
        rows = iota((TILE, 2 * tok_rows), 0)
        is0, is1 = rows == id0, rows == id1
        chosen = onehot(is0 | is1)[:, :tok_rows]
        before = jnp.dot(chosen, earlier, preferred_element_type=F32)
        slot0 = jnp.sum(jnp.where(is0, before, 0.0), axis=0, keepdims=True).astype(I32)
        slot1 = jnp.sum(jnp.where(is1, before, 0.0), axis=0, keepdims=True).astype(I32)
        return id0, id1, slot0, slot1

    def picks_of(found):
        id0, id1, slot0, slot1 = [v[:, :tok_rows] for v in found]
        place = iota((BLOCKS * TILE, tok_rows), 0)
        block, within = place // TILE, place % TILE
        expert_of = ((x + block // 4) % 2) * 4 + (y + block % 4) % 4
        in0, in1 = id0 == expert_of, id1 == expert_of
        last = TILE + within % EXTRA
        main = onehot((in0 & (slot0 == within)) | (in1 & (slot1 == within)))
        rest = (in0 & (slot0 == last)) | (in1 & (slot1 == last))
        return main, [onehot(rest & (within // EXTRA == g)) for g in range(GROUPS)]

    def fill(dst, picks, src, first, cols):
        main, rest = picks
        fold = cols // GROUPS
        dst[:, 0:cols] = jnp.dot(main, src[:, first:first + cols], preferred_element_type=F32).astype(BF16)
        extra = jnp.zeros((BLOCKS * TILE, fold), F32)
        for g in range(GROUPS):
            extra += jnp.dot(rest[g], src[:, first + g * fold:first + (g + 1) * fold], preferred_element_type=F32)
        dst[:, cols:cols + fold] = extra.astype(BF16)

    meta_ref = meta_v.at[0]
    meta_v[0] = jnp.zeros((8, 2 * tok_rows), F32)
    for at in (slice(0, tok_rows), slice(tok_rows, 2 * tok_rows)):
        meta_v[0, 0:2, at] = ids_ref[...].astype(F32)
        meta_v[0, 2:4, at] = rw_ref[...]
    own_slots = slots_of(meta_ref[...])
    own_picks = picks_of(own_slots)
    fill(sendp_v, own_picks, tok_ref, 0, cols_p)

    pl.semaphore_wait(barrier, len(greeted))

    tok_copies = [None] + [
        link(tok_ref.at[:, pl.ds(cols_p, cols_z)], tok_v.at[4 - j], sem_ts.at[j], sem_tr.at[4 - j], planes[j]) for j in (1, 2, 3)]
    meta_copies = [None] + [
        link(meta_ref, meta_v.at[4 - j], sem_ms.at[j], sem_mr.at[4 - j], planes[j]) for j in (1, 2, 3)]
    for j in (1, 3, 2):
        meta_copies[j].start()
        tok_copies[j].start()

    def from_block(r):
        dx, dy = OFFSETS[r]
        return pl.ds(((dx % 2) * 4 + dy) * TILE, TILE)

    def at_block(r):
        return pl.ds(r * TILE, TILE)

    keep = pltpu.make_async_copy(sendp_v.at[from_block(0)], xp_v.at[0, at_block(0)], sem_self.at[0])
    keep.start()
    out_copies = [
        link(sendp_v.at[from_block(r)], xp_v.at[0, at_block(r)], sem_ps.at[r], sem_pr.at[r], peers[r]) for r in range(1, PEERS)]
    for k in PIECE_ORDER:
        for r in offsets_of(k):
            if r:
                out_copies[r - 1].start()

    keep_z = [pltpu.make_async_copy(sendz_v.at[j, from_block(0)], xz_v.at[batch_of(j, 0), at_block(0)], sem_selfz.at[0, j]) for j in range(4)]
    out_z = [
        [link(sendz_v.at[j, from_block(r)], xz_v.at[batch_of(j, r * PIECES // PEERS), at_block(r)], sem_zs.at[j, r], sem_zr.at[j, r], peers[r])
         for r in range(1, PEERS)] for j in range(4)]

    def spread_z(j, picks, src, first):
        fill(sendz_v.at[j], picks, src, first, cols_z)
        for k in PIECE_ORDER:
            for r in offsets_of(k):
                (out_z[j][r - 1] if r else keep_z[j]).start()

    twin_copies = [
        link(src, dst.at[pl.ds(units, units)], sem_ws.at[i], sem_wr.at[i], twin)
        for i, (src, dst) in enumerate(((up_ref, up_v), (down_ref, down_v)))]
    for copy in twin_copies:
        copy.start()

    out_row, in_row = iota((PLANE, PLANE), 0), iota((PLANE, PLANE), 1)
    perm_v[...] = onehot(in_row == (out_row % REST) // EXTRA * TILE + out_row // REST * EXTRA + out_row % EXTRA)
    permt_v[...] = onehot(out_row == (in_row % REST) // EXTRA * TILE + in_row // REST * EXTRA + in_row % EXTRA)

    def piece(k):
        return pl.ds(k * PIECE, PIECE)

    def xp_at(j, k):
        return xp_v.at[batch_of(j, k), piece(k)]

    def yp_at(j, k):
        return yp_v.at[batch_of(j, k), piece(k)]

    up_copies = [link(xp_at(0, k), xp_at(3, k), sem_as.at[0, k], sem_ar.at[0, k], above) for k in range(PIECES)]
    down_copies = [link(xp_at(0, k), xp_at(1, k), sem_as.at[1, k], sem_ar.at[1, k], below) for k in range(PIECES)]
    on_down = {k: link(xp_at(1, k), xp_at(2, k), sem_fs.at[k], sem_fr.at[k], below) for k in WAY_A}
    on_up = {k: link(xp_at(3, k), xp_at(2, k), sem_fs.at[k], sem_fr.at[k], above) for k in WAY_B}

    slots = [own_slots, None, None, None]
    for k, j in zip(PIECE_ORDER, (1, None, 3, None, 0, None, 2, None)):
        if j is None:
            pass
        elif j:
            meta_copies[4 - j].wait_recv()
            tok_copies[4 - j].wait_recv()
            slots[j] = slots_of(meta_v[j])
            spread_z(j, picks_of(slots[j]), tok_v.at[j], 0)
        else:
            spread_z(0, own_picks, tok_ref, cols_p)
        for r in offsets_of(k):
            if r == 0:
                keep.wait()
            else:
                out_copies[r - 1].wait_recv()
        (down_copies if k in WAY_A else up_copies)[k].start()
        if k == 0:
            up_copies[0].start()
    for k in WAY_B:
        down_copies[k].start()
    for k in WAY_A[1:]:
        up_copies[k].start()

    parts = ((xp_v, yp_v, fold_p, cols_p), (xz_v, yz_v, fold_z, cols_z))

    def unfold(j):
        for x_v, _, fold, cols in parts:
            moved = jnp.dot(perm_v[...], x_v[j, 0:PLANE, cols:], preferred_element_type=F32).astype(BF16)
            for g in range(GROUPS):
                x_v[j, PLANE:ROWS, g * fold:(g + 1) * fold] = moved[g * REST:(g + 1) * REST]

    def refold(j, part):
        _, y_v, fold, cols = parts[part]
        total = jnp.zeros((PLANE, fold), F32)
        for g in range(GROUPS):
            total += jnp.dot(permt_v[:, g * REST:(g + 1) * REST], y_v[j, PLANE:ROWS, g * fold:(g + 1) * fold],
                             preferred_element_type=F32)
        y_v[j, 0:PLANE, cols:] = total.astype(BF16)

    def into_hidden(j):
        def body(n, carry):
            at = pl.ds(pl.multiple_of(n * TILE_N, TILE_N), TILE_N)
            v = lax.dot_general(xp_v[j, :, :cols_p], up_v[at, :cols_p], LAST_COLS, preferred_element_type=F32)
            v += lax.dot_general(xz_v[j, :, :cols_z], up_v[at, cols_p:], LAST_COLS, preferred_element_type=F32)
            hid_v[:, at] = (v / (1.0 + jnp.exp(-v))).astype(BF16)
            return carry

        lax.fori_loop(0, 2 * units // TILE_N, body, 0)

    def out_of_hidden(j, part):
        _, y_v, _, cols = parts[part]
        start = part * cols_p

        def body(n, carry):
            at = pl.ds(pl.multiple_of(n * TILE_N, TILE_N), TILE_N)
            down_at = pl.ds(pl.multiple_of(start + n * TILE_N, TILE_N), TILE_N)
            y_v[j, :, at] = jnp.dot(hid_v[...], down_v[:, down_at], preferred_element_type=F32).astype(BF16)
            return carry

        lax.fori_loop(0, cols // TILE_N, body, 0)
        refold(j, part)

    backz_keep = [pltpu.make_async_copy(yz_v.at[batch_of(j, 0), at_block(0)], backz_v.at[j, at_block(0)], sem_selfz.at[1, j]) for j in range(4)]
    backz_copies = [
        [link(yz_v.at[batch_of(j, r * PIECES // PEERS), at_block(r)], backz_v.at[j, at_block(r)], sem_ys.at[j, r], sem_yr.at[j, r], backs[r])
         for r in range(1, PEERS)] for j in range(4)]

    def return_z(batch):
        out_of_hidden(batch, 1)
        for j, k in pairs_of(batch):
            for r in offsets_of(k):
                (backz_copies[j][r - 1] if r else backz_keep[j]).start()

    def enter(batch):
        for j, k in pairs_of(batch):
            for r in offsets_of(k):
                if r:
                    out_z[j][r - 1].wait_recv()
                else:
                    keep_z[j].wait()
        unfold(batch)
        into_hidden(batch)
        out_of_hidden(batch, 0)

    to_above = [link(yp_at(1, k), from_down.at[piece(k)], sem_1s.at[0, k], sem_1r.at[0, k], above) for k in range(PIECES)]
    to_below = [link(yp_at(3, k), from_up.at[piece(k)], sem_1s.at[1, k], sem_1r.at[1, k], below) for k in range(PIECES)]
    far_below = {k: link(yp_at(2, k), far_v.at[piece(k)], sem_2s.at[k], sem_2r.at[k], below) for k in WAY_A}
    far_above = {k: link(yp_at(2, k), far_v.at[piece(k)], sem_2s.at[k], sem_2r.at[k], above) for k in WAY_B}

    for a, b in zip(WAY_A, WAY_B):
        down_copies[a].wait_recv()
        on_down[a].start()
        up_copies[b].wait_recv()
        on_up[b].start()
    own_up.wait()
    twin_copies[0].wait_recv()
    own_down.wait()
    twin_copies[1].wait_recv()
    enter(1)
    return_z(1)
    for a, b in zip(WAY_A, WAY_B):
        down_copies[b].wait_recv()
        up_copies[a].wait_recv()
    for a, b in zip(WAY_A, WAY_B):
        to_above[a].start()
        to_below[b].start()
    enter(3)
    return_z(3)
    for a, b in zip(WAY_A, WAY_B):
        on_down[a].wait_recv()
        on_up[b].wait_recv()
    enter(2)
    for a, b in zip(WAY_A, WAY_B):
        far_below[a].start()
        far_above[b].start()
    return_z(2)

    place = iota((PLANE, 2 * tok_rows), 0)
    block, within = place // TILE, place % TILE
    dx, dy = jnp.zeros_like(place), jnp.zeros_like(place)
    for r, (rx, ry) in enumerate(OFFSETS):
        dx, dy = jnp.where(block == r, rx, dx), jnp.where(block == r, ry, dy)
    expert_of = ((x + dx) % 2) * 4 + (y + dy) % 4
    is_high = iota((PLANE, 2 * tok_rows), 1) < tok_rows

    def weigh(found, meta, slot):
        id0, id1, slot0, slot1 = found
        full = (jnp.where((id0 == expert_of) & (slot0 == slot), meta[2:3], 0.0)
                + jnp.where((id1 == expert_of) & (slot1 == slot), meta[3:4], 0.0))
        high = full.astype(BF16).astype(F32)
        return jnp.where(is_high, high, full - high)

    def combine(found, meta, src, cols, put):
        fold = cols // GROUPS
        main = weigh(found, meta, within).astype(BF16)
        rest = weigh(found, meta, TILE + within % EXTRA)
        for g in range(GROUPS):
            at = slice(g * fold, (g + 1) * fold)
            both = lax.dot_general(main, src[:, at], FIRST_ROWS, preferred_element_type=F32)
            both += lax.dot_general(jnp.where(within // EXTRA == g, rest, 0.0).astype(BF16), src[:, cols:],
                                    FIRST_ROWS, preferred_element_type=F32)
            put(at, both[:tok_rows] + both[tok_rows:])

    part_copies = [None] + [link(part_v.at[j], got_v.at[j], sem_gs.at[j], sem_gr.at[j], planes[j]) for j in (1, 2, 3)]

    def gather_z(j):
        backz_keep[j].wait()
        for copy in backz_copies[j]:
            copy.wait_recv()

        def put(at, value):
            part_v[j, :, at] = value.astype(BF16)

        combine(slots[j], meta_ref[...] if j == 0 else meta_v[j], backz_v.at[j], cols_z, put)
        if j:
            part_copies[j].start()

    gather_z(1)
    enter(0)
    return_z(0)

    def add_into(target, j, k, others):
        total = target[j, piece(k), :].astype(F32)
        for other in others:
            total += other[piece(k), :].astype(F32)
        target[j, piece(k), :] = total.astype(BF16)

    for a, b, j in zip(WAY_A, WAY_B, (None, 3, None, 2)):
        far_below[a].wait_recv()
        add_into(yp_v, 3, a, (far_v,))
        to_below[a].start()
        far_above[b].wait_recv()
        add_into(yp_v, 3, b, (far_v,))
        to_above[b].start()
        if j:
            gather_z(j)
    gather_z(0)

    back_keep = pltpu.make_async_copy(yp_v.at[0, at_block(0)], backp_v.at[at_block(0)], sem_self.at[1])
    back_copies = [
        link(yp_v.at[0, at_block(r)], backp_v.at[at_block(r)], sem_bs.at[r], sem_br.at[r], backs[r]) for r in range(1, PEERS)]
    for k in PIECE_ORDER:
        to_above[k].wait_recv()
        to_below[k].wait_recv()
        add_into(yp_v, 0, k, (from_up, from_down))
        for r in offsets_of(k):
            (back_keep if r == 0 else back_copies[r - 1]).start()

    for j in (1, 2, 3):
        part_copies[j].wait_recv()
    total = part_v[0].astype(F32)
    for j in (1, 2, 3):
        total += got_v[j].astype(F32)
    out_ref[:, cols_p:] = total.astype(BF16)

    back_keep.wait()
    for copy in back_copies:
        copy.wait_recv()

    def put_out(at, value):
        out_ref[:, at] = value.astype(BF16)

    combine(own_slots, meta_ref[...], backp_v, cols_p, put_out)

    onward = [way[k] for way in (on_up, on_down, far_below, far_above) for k in sorted(way)]
    for copy in (out_copies + twin_copies + up_copies + down_copies + to_above + to_below + onward + back_copies + tok_copies[1:] + meta_copies[1:] + part_copies[1:]):
        copy.wait_send()
    for j in range(4):
        for copy in out_z[j] + backz_copies[j]:
            copy.wait_send()


def shards(tokens, expert_ids, route_weights, up_weight, down_weight):
    tok_rows, features = tokens.shape
    units = up_weight.shape[1]
    cols_z = features // 3
    cols_p = features - cols_z
    wide_p, wide_z = cols_p + cols_p // GROUPS, cols_z + cols_z // GROUPS
    vmem = pl.BlockSpec(memory_space=pltpu.VMEM)
    anywhere = pl.BlockSpec(memory_space=pl.ANY)
    dma = pltpu.SemaphoreType.DMA
    return pl.pallas_call(
        kernel,
        out_shape=jax.ShapeDtypeStruct((tok_rows, features), BF16),
        in_specs=[vmem, vmem, vmem, anywhere, anywhere],
        out_specs=vmem,
        scratch_shapes=[
            pltpu.VMEM((2 * units, features), BF16),
            pltpu.VMEM((2 * units, features), BF16),
            pltpu.VMEM((4, ROWS, wide_p), BF16),
            pltpu.VMEM((4, ROWS, wide_z), BF16),
            pltpu.VMEM((4, ROWS, wide_p), BF16),
            pltpu.VMEM((4, ROWS, wide_z), BF16),
            pltpu.VMEM((PLANE, wide_p), BF16),
            pltpu.VMEM((PLANE, wide_p), BF16),
            pltpu.VMEM((PLANE, wide_p), BF16),
            pltpu.VMEM((PLANE, wide_p), BF16),
            pltpu.VMEM((4, PLANE, wide_z), BF16),
            pltpu.VMEM((BLOCKS * TILE, wide_p), BF16),
            pltpu.VMEM((4, BLOCKS * TILE, wide_z), BF16),
            pltpu.VMEM((4, tok_rows, cols_z), BF16),
            pltpu.VMEM((4, 8, 2 * tok_rows), F32),
            pltpu.VMEM((4, tok_rows, cols_z), BF16),
            pltpu.VMEM((4, tok_rows, cols_z), BF16),
            pltpu.VMEM((ROWS, 2 * units), BF16),
            pltpu.VMEM((PLANE, PLANE), BF16),
            pltpu.VMEM((PLANE, PLANE), BF16),
            dma((2,)), dma((2,)), dma((2,)), dma((2,)), dma((2, 4)),
            dma((PEERS,)), dma((PEERS,)),
            dma((2, PIECES)), dma((2, PIECES)), dma((PIECES,)), dma((PIECES,)),
            dma((PIECES,)), dma((PIECES,)), dma((2, PIECES)), dma((2, PIECES)),
            dma((PEERS,)), dma((PEERS,)),
            dma((4,)), dma((4,)), dma((4,)), dma((4,)),
            dma((4, PEERS)), dma((4, PEERS)), dma((4, PEERS)), dma((4, PEERS)), dma((4,)), dma((4,)),
        ],
        compiler_params=pltpu.CompilerParams(
            collective_id=0, has_side_effects=True, vmem_limit_bytes=63 * 2**20),
        cost_estimate=pl.CostEstimate(
            flops=4 * 4 * ROWS * 2 * units * features, bytes_accessed=6 * units * features, transcendentals=0),
    )(tokens, expert_ids.T, route_weights.T, up_weight[0], down_weight[0])


def solution(mesh):
    return jax.shard_map(
        shards,
        mesh=mesh,
        in_specs=(
            P(("expert", "fsdp"), None),
            P(("expert", "fsdp"), None),
            P(("expert", "fsdp"), None),
            P("expert", "fsdp", None),
            P("expert", "fsdp", None),
        ),
        out_specs=P(("expert", "fsdp"), None),
        check_vma=False,
    )
```

```python
import jax
import jax.numpy as jnp
from jax import lax
from jax.experimental import pallas as pl
from jax.experimental.pallas import tpu as pltpu
from jax.sharding import PartitionSpec as P

MESH = pl.DeviceIdType.MESH
BF16, F32, I32 = jnp.bfloat16, jnp.float32, jnp.int32

OFFSETS = (
    (0, 0), (1, 1), (3, 3), (2, 2),
    (1, 2), (3, 2), (2, 1), (2, 3),
    (1, 3), (3, 1), (2, 0), (0, 2),
    (1, 0), (3, 0), (0, 1), (0, 3),
)
PIECE_ORDER = (0, 4, 1, 5, 2, 6, 3, 7)
PEERS = len(OFFSETS)
BLOCKS = 8
TILE = 16
EXTRA = 2
GROUPS = TILE // EXTRA
PIECES = 8
PIECE = PEERS // PIECES * TILE
PLANE = PEERS * TILE
REST = PEERS * EXTRA
ROWS = PLANE + REST
TILE_N = 1024
WAY_A, WAY_B = (0, 1, 2, 3), (4, 5, 6, 7)
FIRST_ROWS = (((0,), (0,)), ((), ()))
LAST_COLS = (((1,), (1,)), ((), ()))


def batch_of(j, k):
    return j if j % 2 == 0 or k in WAY_A else 4 - j


def pairs_of(batch):
    return [(j, k) for j in range(4) for k in range(PIECES) if batch_of(j, k) == batch]


def offsets_of(k):
    return range(k * PEERS // PIECES, (k + 1) * PEERS // PIECES)


def iota(shape, dim):
    return lax.broadcasted_iota(I32, shape, dim)


def onehot(mask):
    return jnp.where(mask, 1.0, 0.0).astype(BF16)


def kernel(
    tok_ref, ids_ref, rw_ref, up_ref, down_ref, out_ref,
    up_v, down_v, xp_v, xz_v, yp_v, yz_v, from_up, from_down, far_v, backp_v, backz_v, sendp_v, sendz_v,
    tok_v, meta_v, part_v, got_v, hid_v, perm_v, permt_v,
    sem_w, sem_ws, sem_wr, sem_self, sem_selfz, sem_ps, sem_pr, sem_as, sem_ar, sem_fs, sem_fr,
    sem_2s, sem_2r, sem_1s, sem_1r, sem_bs, sem_br,
    sem_ts, sem_tr, sem_ms, sem_mr, sem_zs, sem_zr, sem_ys, sem_yr, sem_gs, sem_gr,
):
    tok_rows, features = tok_ref.shape
    units = up_ref.shape[0]
    cols_z = tok_v.shape[2]
    cols_p = features - cols_z
    fold_p, fold_z = cols_p // GROUPS, cols_z // GROUPS
    e, f = lax.axis_index("expert"), lax.axis_index("fsdp")
    x_lo, y = e // 4, e % 4
    z, x_hi, core = f // 4, (f // 2) % 2, f % 2
    x = x_hi * 2 + x_lo

    def device(dx, dy, dz=0, dc=0):
        px, py, pz, pc = (x + dx) % 4, (y + dy) % 4, (z + dz) % 4, (core + dc) % 2
        return {"expert": (px % 2) * 4 + py, "fsdp": (pz * 2 + px // 2) * 2 + pc}

    peers = [device(dx, dy) for dx, dy in OFFSETS]
    backs = [device(-dx, -dy) for dx, dy in OFFSETS]
    planes = [None] + [device(0, 0, j) for j in (1, 2, 3)]
    above, below, twin = planes[1], planes[3], device(0, 0, 0, 1)

    barrier = pltpu.get_barrier_semaphore()
    farthest = sorted(range(1, PEERS), key=lambda r: -sum(min(d, 4 - d) for d in OFFSETS[r]))
    greeted = [planes[2]] + [peers[r] for r in farthest] + [above, below, twin]
    for other in greeted:
        pl.semaphore_signal(barrier, inc=1, device_id=other, device_id_type=MESH)

    def link(src, dst, send, recv, to):
        return pltpu.make_async_remote_copy(
            src_ref=src, dst_ref=dst, send_sem=send, recv_sem=recv, device_id=to, device_id_type=MESH)

    own_up = pltpu.make_async_copy(up_ref, up_v.at[pl.ds(0, units)], sem_w.at[0])
    own_down = pltpu.make_async_copy(down_ref, down_v.at[pl.ds(0, units)], sem_w.at[1])
    own_up.start()
    own_down.start()

    lane_tok = iota((tok_rows, 2 * tok_rows), 1) % tok_rows
    earlier = onehot(iota((tok_rows, 2 * tok_rows), 0) < lane_tok)

    def slots_of(meta):
        id0, id1 = meta[0:1].astype(I32), meta[1:2].astype(I32)
        rows = iota((TILE, 2 * tok_rows), 0)
        is0, is1 = rows == id0, rows == id1
        chosen = onehot(is0 | is1)[:, :tok_rows]
        before = jnp.dot(chosen, earlier, preferred_element_type=F32)
        slot0 = jnp.sum(jnp.where(is0, before, 0.0), axis=0, keepdims=True).astype(I32)
        slot1 = jnp.sum(jnp.where(is1, before, 0.0), axis=0, keepdims=True).astype(I32)
        return id0, id1, slot0, slot1

    def picks_of(found):
        id0, id1, slot0, slot1 = [v[:, :tok_rows] for v in found]
        place = iota((BLOCKS * TILE, tok_rows), 0)
        block, within = place // TILE, place % TILE
        expert_of = ((x + block // 4) % 2) * 4 + (y + block % 4) % 4
        in0, in1 = id0 == expert_of, id1 == expert_of
        last = TILE + within % EXTRA
        main = onehot((in0 & (slot0 == within)) | (in1 & (slot1 == within)))
        rest = (in0 & (slot0 == last)) | (in1 & (slot1 == last))
        return main, [onehot(rest & (within // EXTRA == g)) for g in range(GROUPS)]

    def fill(dst, picks, src, first, cols):
        main, rest = picks
        fold = cols // GROUPS
        dst[:, 0:cols] = jnp.dot(main, src[:, first:first + cols], preferred_element_type=F32).astype(BF16)
        extra = jnp.zeros((BLOCKS * TILE, fold), F32)
        for g in range(GROUPS):
            extra += jnp.dot(rest[g], src[:, first + g * fold:first + (g + 1) * fold], preferred_element_type=F32)
        dst[:, cols:cols + fold] = extra.astype(BF16)

    meta_ref = meta_v.at[0]
    meta_v[0] = jnp.zeros((8, 2 * tok_rows), F32)
    for at in (slice(0, tok_rows), slice(tok_rows, 2 * tok_rows)):
        meta_v[0, 0:2, at] = ids_ref[...].astype(F32)
        meta_v[0, 2:4, at] = rw_ref[...]
    own_slots = slots_of(meta_ref[...])
    own_picks = picks_of(own_slots)
    fill(sendp_v, own_picks, tok_ref, 0, cols_p)

    pl.semaphore_wait(barrier, len(greeted))

    tok_copies = [None] + [
        link(tok_ref.at[:, pl.ds(cols_p, cols_z)], tok_v.at[4 - j], sem_ts.at[j], sem_tr.at[4 - j], planes[j]) if j != 2 else None
        for j in (1, 2, 3)]
    half = cols_z // 2
    tok_on = {j: link(tok_v.at[j, :, pl.ds(at, half)], tok_v.at[2, :, pl.ds(at, half)], sem_ts.at[j - 1], sem_tr.at[j - 1], planes[4 - j])
              for j, at in ((1, 0), (3, half))}
    meta_copies = [None] + [
        link(meta_ref, meta_v.at[4 - j], sem_ms.at[j], sem_mr.at[4 - j], planes[j]) for j in (1, 2, 3)]
    for j in (1, 3, 2):
        meta_copies[j].start()
        if j != 2:
            tok_copies[j].start()

    def from_block(r):
        dx, dy = OFFSETS[r]
        return pl.ds(((dx % 2) * 4 + dy) * TILE, TILE)

    def at_block(r):
        return pl.ds(r * TILE, TILE)

    keep = pltpu.make_async_copy(sendp_v.at[from_block(0)], xp_v.at[0, at_block(0)], sem_self.at[0])
    keep.start()
    out_copies = [
        link(sendp_v.at[from_block(r)], xp_v.at[0, at_block(r)], sem_ps.at[r], sem_pr.at[r], peers[r]) for r in range(1, PEERS)]
    for k in PIECE_ORDER:
        for r in offsets_of(k):
            if r:
                out_copies[r - 1].start()

    keep_z = [pltpu.make_async_copy(sendz_v.at[j, from_block(0)], xz_v.at[batch_of(j, 0), at_block(0)], sem_selfz.at[0, j]) for j in range(4)]
    out_z = [
        [link(sendz_v.at[j, from_block(r)], xz_v.at[batch_of(j, r * PIECES // PEERS), at_block(r)], sem_zs.at[j, r], sem_zr.at[j, r], peers[r])
         for r in range(1, PEERS)] for j in range(4)]

    def spread_z(j, picks, src, first):
        fill(sendz_v.at[j], picks, src, first, cols_z)
        for k in PIECE_ORDER:
            for r in offsets_of(k):
                (out_z[j][r - 1] if r else keep_z[j]).start()

    twin_copies = [
        link(src, dst.at[pl.ds(units, units)], sem_ws.at[i], sem_wr.at[i], twin)
        for i, (src, dst) in enumerate(((up_ref, up_v), (down_ref, down_v)))]
    for copy in twin_copies:
        copy.start()

    out_row, in_row = iota((PLANE, PLANE), 0), iota((PLANE, PLANE), 1)
    perm_v[...] = onehot(in_row == (out_row % REST) // EXTRA * TILE + out_row // REST * EXTRA + out_row % EXTRA)
    permt_v[...] = onehot(out_row == (in_row % REST) // EXTRA * TILE + in_row // REST * EXTRA + in_row % EXTRA)

    def piece(k):
        return pl.ds(k * PIECE, PIECE)

    def xp_at(j, k):
        return xp_v.at[batch_of(j, k), piece(k)]

    def yp_at(j, k):
        return yp_v.at[batch_of(j, k), piece(k)]

    up_copies = [link(xp_at(0, k), xp_at(3, k), sem_as.at[0, k], sem_ar.at[0, k], above) for k in range(PIECES)]
    down_copies = [link(xp_at(0, k), xp_at(1, k), sem_as.at[1, k], sem_ar.at[1, k], below) for k in range(PIECES)]
    on_down = {k: link(xp_at(1, k), xp_at(2, k), sem_fs.at[k], sem_fr.at[k], below) for k in WAY_A}
    on_up = {k: link(xp_at(3, k), xp_at(2, k), sem_fs.at[k], sem_fr.at[k], above) for k in WAY_B}

    slots = [own_slots, None, None, None]
    for k, j in zip(PIECE_ORDER, (1, None, 3, None, 0, None, 2, None)):
        if j is None:
            pass
        elif j:
            meta_copies[4 - j].wait_recv()
            if j == 2:
                tok_on[1].wait_recv()
                tok_on[3].wait_recv()
            else:
                tok_copies[4 - j].wait_recv()
                tok_on[j].start()
            slots[j] = slots_of(meta_v[j])
            spread_z(j, picks_of(slots[j]), tok_v.at[j], 0)
        else:
            spread_z(0, own_picks, tok_ref, cols_p)
        for r in offsets_of(k):
            if r == 0:
                keep.wait()
            else:
                out_copies[r - 1].wait_recv()
        (down_copies if k in WAY_A else up_copies)[k].start()
        if k == 0:
            up_copies[0].start()
    for k in WAY_B:
        down_copies[k].start()
    for k in WAY_A[1:]:
        up_copies[k].start()

    parts = ((xp_v, yp_v, fold_p, cols_p), (xz_v, yz_v, fold_z, cols_z))

    def unfold(j):
        for x_v, _, fold, cols in parts:
            moved = jnp.dot(perm_v[...], x_v[j, 0:PLANE, cols:], preferred_element_type=F32).astype(BF16)
            for g in range(GROUPS):
                x_v[j, PLANE:ROWS, g * fold:(g + 1) * fold] = moved[g * REST:(g + 1) * REST]

    def refold(j, part):
        _, y_v, fold, cols = parts[part]
        total = jnp.zeros((PLANE, fold), F32)
        for g in range(GROUPS):
            total += jnp.dot(permt_v[:, g * REST:(g + 1) * REST], y_v[j, PLANE:ROWS, g * fold:(g + 1) * fold],
                             preferred_element_type=F32)
        y_v[j, 0:PLANE, cols:] = total.astype(BF16)

    def into_hidden(j):
        def body(n, carry):
            at = pl.ds(pl.multiple_of(n * TILE_N, TILE_N), TILE_N)
            v = lax.dot_general(xp_v[j, :, :cols_p], up_v[at, :cols_p], LAST_COLS, preferred_element_type=F32)
            v += lax.dot_general(xz_v[j, :, :cols_z], up_v[at, cols_p:], LAST_COLS, preferred_element_type=F32)
            hid_v[:, at] = (v / (1.0 + jnp.exp(-v))).astype(BF16)
            return carry

        lax.fori_loop(0, 2 * units // TILE_N, body, 0)

    def out_of_hidden(j, part):
        _, y_v, _, cols = parts[part]
        start = part * cols_p

        def body(n, carry):
            at = pl.ds(pl.multiple_of(n * TILE_N, TILE_N), TILE_N)
            down_at = pl.ds(pl.multiple_of(start + n * TILE_N, TILE_N), TILE_N)
            y_v[j, :, at] = jnp.dot(hid_v[...], down_v[:, down_at], preferred_element_type=F32).astype(BF16)
            return carry

        lax.fori_loop(0, cols // TILE_N, body, 0)
        refold(j, part)

    backz_keep = [pltpu.make_async_copy(yz_v.at[batch_of(j, 0), at_block(0)], backz_v.at[j, at_block(0)], sem_selfz.at[1, j]) for j in range(4)]
    backz_copies = [
        [link(yz_v.at[batch_of(j, r * PIECES // PEERS), at_block(r)], backz_v.at[j, at_block(r)], sem_ys.at[j, r], sem_yr.at[j, r], backs[r])
         for r in range(1, PEERS)] for j in range(4)]

    def return_z(batch):
        out_of_hidden(batch, 1)
        for j, k in pairs_of(batch):
            for r in offsets_of(k):
                (backz_copies[j][r - 1] if r else backz_keep[j]).start()

    def enter(batch):
        for j, k in pairs_of(batch):
            for r in offsets_of(k):
                if r:
                    out_z[j][r - 1].wait_recv()
                else:
                    keep_z[j].wait()
        unfold(batch)
        into_hidden(batch)
        out_of_hidden(batch, 0)

    to_above = [link(yp_at(1, k), from_down.at[piece(k)], sem_1s.at[0, k], sem_1r.at[0, k], above) for k in range(PIECES)]
    to_below = [link(yp_at(3, k), from_up.at[piece(k)], sem_1s.at[1, k], sem_1r.at[1, k], below) for k in range(PIECES)]
    far_below = {k: link(yp_at(2, k), far_v.at[piece(k)], sem_2s.at[k], sem_2r.at[k], below) for k in WAY_A}
    far_above = {k: link(yp_at(2, k), far_v.at[piece(k)], sem_2s.at[k], sem_2r.at[k], above) for k in WAY_B}

    for a, b in zip(WAY_A, WAY_B):
        down_copies[a].wait_recv()
        on_down[a].start()
        up_copies[b].wait_recv()
        on_up[b].start()
    own_up.wait()
    twin_copies[0].wait_recv()
    own_down.wait()
    twin_copies[1].wait_recv()
    enter(1)
    return_z(1)
    for a, b in zip(WAY_A, WAY_B):
        down_copies[b].wait_recv()
        up_copies[a].wait_recv()
    for a, b in zip(WAY_A, WAY_B):
        to_above[a].start()
        to_below[b].start()
    enter(3)
    return_z(3)
    for a, b in zip(WAY_A, WAY_B):
        on_down[a].wait_recv()
        on_up[b].wait_recv()
    enter(2)
    for a, b in zip(WAY_A, WAY_B):
        far_below[a].start()
        far_above[b].start()
    return_z(2)

    place = iota((PLANE, 2 * tok_rows), 0)
    block, within = place // TILE, place % TILE
    dx, dy = jnp.zeros_like(place), jnp.zeros_like(place)
    for r, (rx, ry) in enumerate(OFFSETS):
        dx, dy = jnp.where(block == r, rx, dx), jnp.where(block == r, ry, dy)
    expert_of = ((x + dx) % 2) * 4 + (y + dy) % 4
    is_high = iota((PLANE, 2 * tok_rows), 1) < tok_rows

    def weigh(found, meta, slot):
        id0, id1, slot0, slot1 = found
        full = (jnp.where((id0 == expert_of) & (slot0 == slot), meta[2:3], 0.0)
                + jnp.where((id1 == expert_of) & (slot1 == slot), meta[3:4], 0.0))
        high = full.astype(BF16).astype(F32)
        return jnp.where(is_high, high, full - high)

    def weights_of(found, meta):
        rest = weigh(found, meta, TILE + within % EXTRA)
        return weigh(found, meta, within).astype(BF16), [
            jnp.where(within // EXTRA == g, rest, 0.0).astype(BF16) for g in range(GROUPS)]

    def combine(weights, src, cols, put):
        main, rest = weights
        fold = cols // GROUPS
        for g in range(GROUPS):
            at = slice(g * fold, (g + 1) * fold)
            both = lax.dot_general(main, src[:, at], FIRST_ROWS, preferred_element_type=F32)
            both += lax.dot_general(rest[g], src[:, cols:], FIRST_ROWS, preferred_element_type=F32)
            put(at, both[:tok_rows] + both[tok_rows:])

    part_copies = [None] + [link(part_v.at[j], got_v.at[j], sem_gs.at[j], sem_gr.at[j], planes[j]) for j in (1, 2, 3)]

    def gather_z(j):
        weights = own_weights if j == 0 else weights_of(slots[j], meta_v[j])
        backz_keep[j].wait()
        for copy in backz_copies[j]:
            copy.wait_recv()

        def put(at, value):
            part_v[j, :, at] = value.astype(BF16)

        combine(weights, backz_v.at[j], cols_z, put)
        if j:
            part_copies[j].start()

    gather_z(1)
    enter(0)
    return_z(0)

    def add_into(target, j, k, others):
        total = target[j, piece(k), :].astype(F32)
        for other in others:
            total += other[piece(k), :].astype(F32)
        target[j, piece(k), :] = total.astype(BF16)

    for a, b, j in zip(WAY_A, WAY_B, (None, 3, None, 2)):
        far_below[a].wait_recv()
        add_into(yp_v, 3, a, (far_v,))
        to_below[a].start()
        far_above[b].wait_recv()
        add_into(yp_v, 3, b, (far_v,))
        to_above[b].start()
        if j:
            gather_z(j)
    own_weights = weights_of(own_slots, meta_ref[...])

    back_keep = pltpu.make_async_copy(yp_v.at[0, at_block(0)], backp_v.at[at_block(0)], sem_self.at[1])
    back_copies = [
        link(yp_v.at[0, at_block(r)], backp_v.at[at_block(r)], sem_bs.at[r], sem_br.at[r], backs[r]) for r in range(1, PEERS)]
    for k in PIECE_ORDER:
        to_above[k].wait_recv()
        to_below[k].wait_recv()
        add_into(yp_v, 0, k, (from_up, from_down))
        for r in offsets_of(k):
            (back_keep if r == 0 else back_copies[r - 1]).start()
        if k == PIECE_ORDER[PIECES // 2 - 1]:
            gather_z(0)

    for j in (1, 2, 3):
        part_copies[j].wait_recv()
    total = part_v[0].astype(F32)
    for j in (1, 2, 3):
        total += got_v[j].astype(F32)
    out_ref[:, cols_p:] = total.astype(BF16)

    back_keep.wait()
    for copy in back_copies:
        copy.wait_recv()

    def put_out(at, value):
        out_ref[:, at] = value.astype(BF16)

    combine(own_weights, backp_v, cols_p, put_out)

    onward = [way[k] for way in (on_up, on_down, far_below, far_above) for k in sorted(way)]
    for copy in (out_copies + twin_copies + up_copies + down_copies + to_above + to_below + onward + back_copies
                 + [tok_copies[1], tok_copies[3], tok_on[1], tok_on[3]] + meta_copies[1:] + part_copies[1:]):
        copy.wait_send()
    for j in range(4):
        for copy in out_z[j] + backz_copies[j]:
            copy.wait_send()


def shards(tokens, expert_ids, route_weights, up_weight, down_weight):
    tok_rows, features = tokens.shape
    units = up_weight.shape[1]
    cols_z = features // 3
    cols_p = features - cols_z
    wide_p, wide_z = cols_p + cols_p // GROUPS, cols_z + cols_z // GROUPS
    vmem = pl.BlockSpec(memory_space=pltpu.VMEM)
    anywhere = pl.BlockSpec(memory_space=pl.ANY)
    dma = pltpu.SemaphoreType.DMA
    return pl.pallas_call(
        kernel,
        out_shape=jax.ShapeDtypeStruct((tok_rows, features), BF16),
        in_specs=[vmem, vmem, vmem, anywhere, anywhere],
        out_specs=vmem,
        scratch_shapes=[
            pltpu.VMEM((2 * units, features), BF16),
            pltpu.VMEM((2 * units, features), BF16),
            pltpu.VMEM((4, ROWS, wide_p), BF16),
            pltpu.VMEM((4, ROWS, wide_z), BF16),
            pltpu.VMEM((4, ROWS, wide_p), BF16),
            pltpu.VMEM((4, ROWS, wide_z), BF16),
            pltpu.VMEM((PLANE, wide_p), BF16),
            pltpu.VMEM((PLANE, wide_p), BF16),
            pltpu.VMEM((PLANE, wide_p), BF16),
            pltpu.VMEM((PLANE, wide_p), BF16),
            pltpu.VMEM((4, PLANE, wide_z), BF16),
            pltpu.VMEM((BLOCKS * TILE, wide_p), BF16),
            pltpu.VMEM((4, BLOCKS * TILE, wide_z), BF16),
            pltpu.VMEM((4, tok_rows, cols_z), BF16),
            pltpu.VMEM((4, 8, 2 * tok_rows), F32),
            pltpu.VMEM((4, tok_rows, cols_z), BF16),
            pltpu.VMEM((4, tok_rows, cols_z), BF16),
            pltpu.VMEM((ROWS, 2 * units), BF16),
            pltpu.VMEM((PLANE, PLANE), BF16),
            pltpu.VMEM((PLANE, PLANE), BF16),
            dma((2,)), dma((2,)), dma((2,)), dma((2,)), dma((2, 4)),
            dma((PEERS,)), dma((PEERS,)),
            dma((2, PIECES)), dma((2, PIECES)), dma((PIECES,)), dma((PIECES,)),
            dma((PIECES,)), dma((PIECES,)), dma((2, PIECES)), dma((2, PIECES)),
            dma((PEERS,)), dma((PEERS,)),
            dma((4,)), dma((4,)), dma((4,)), dma((4,)),
            dma((4, PEERS)), dma((4, PEERS)), dma((4, PEERS)), dma((4, PEERS)), dma((4,)), dma((4,)),
        ],
        compiler_params=pltpu.CompilerParams(
            collective_id=0, has_side_effects=True, vmem_limit_bytes=63 * 2**20),
        cost_estimate=pl.CostEstimate(
            flops=4 * 4 * ROWS * 2 * units * features, bytes_accessed=6 * units * features, transcendentals=0),
    )(tokens, expert_ids.T, route_weights.T, up_weight[0], down_weight[0])


def solution(mesh):
    return jax.shard_map(
        shards,
        mesh=mesh,
        in_specs=(
            P(("expert", "fsdp"), None),
            P(("expert", "fsdp"), None),
            P(("expert", "fsdp"), None),
            P("expert", "fsdp", None),
            P("expert", "fsdp", None),
        ),
        out_specs=P(("expert", "fsdp"), None),
        check_vma=False,
    )
```
